32 devices in a mesh: slab: 8 (over z, y), ang: 4 (over x, core).
Axes of the slice: x: 2, y: 2, z: 4, core: 2. Of those that a mesh axis runs over, the one named last changes fastest.
Arguments:
- conc: bfloat16 [8, 2, 128, 2048], P(None, None, 'slab'), may hold values from 0.049804688 to 1
- spectra: bfloat16 [4, 512, 256], P('ang', 'slab'), may hold values from -4 to 4
- path_slab: int32 [4, 512, 1], P('ang', 'slab'), may hold values from 0 to 7; in each aligned block of 64 rows (0 to 63, 64 to 127, ..., all dimensions but the last counted through in order) at most 16 rows name the same one
- line_offset: int32 [4, 512], P('ang', 'slab'), may hold values from 0 to 31
- profile: float32 [8, 256], replicated, may hold values from 0.01 to 0.3
- beam_absorb: float32 [8], replicated, may hold values from 0.1 to 0.6
- line_absorb: float32 [8, 8], replicated, as said below
Outputs:
- grad_maps: float32 [8, 2, 128, 2048], P(None, None, 'slab', 'ang')
The draws below stay inside these ranges and needn't reach their ends.
Inputs may be any that keep to these rules, and one draw needn't show every extreme that they name: `path_slab`: among the 64 scan points of one view on one device (aligned blocks), no slab is named more than 16 times, a bound that some block reaches. `line_absorb`: positive coefficients.
All inputs are finite; a program needn't handle non-finite values.
Results may differ from the reference program's by a relative error of at most 0.0003.
Values may be sent and summed in bfloat16 or wider, within the bound.
A program may use at most 64 MiB of HBM per device.

```python
import math
import jax
import jax.numpy as jnp
import numpy as np
from jax import lax

E = 8
CH = 256
NC = 2048
VIEWS = 4
SL = 2
ROWS_DEV = 16
BAND = 8
NR = 128
RAYS_DEV = 64
RAYS = 512
CAP = 16
N_SLAB = 8


def draw_line_absorb(key, part):
    base = jnp.exp(jax.random.uniform(key, (E, E), jnp.float32, math.log(0.05), math.log(0.3)))
    diagonal_mask = lax.broadcasted_iota(jnp.int32, (E, E), 0) == lax.broadcasted_iota(jnp.int32, (E, E), 1)
    boost = jnp.where(diagonal_mask, 4.0, 1.0)
    return base * boost / BAND


def place_ends(entries, key, least, top_value):
    place = [jax.random.randint(jax.random.fold_in(key, axis), (), 0, length) for axis, length in enumerate(entries.shape)]
    main_axis = entries.shape.index(max(entries.shape))
    beside = place[:main_axis] + [(place[main_axis] + 1) % entries.shape[main_axis]] + place[main_axis + 1:]
    return entries.at[tuple(place)].set(least).at[tuple(beside)].set(top_value)


def levels(own_key, shape, shards, low, largest):
    def one(dim, parts):
        draws = jax.random.uniform(jax.random.fold_in(jax.random.fold_in(own_key, 6), dim), (parts,), jnp.float32, low / len(shards), largest / len(shards))
        return jnp.repeat(jnp.exp(draws), shape[dim] // parts).reshape((-1,) + (1,) * (len(shape) - dim - 1))

    gain = one(*shards[0])
    for cut in shards[1:]:
        gain = gain * one(*cut)
    return gain


def routed_block(key, own, number, rows, amount, top, bound, slope):
    order = jax.random.permutation(key, amount)
    heavy_load, usual = load_shares(amount, rows * top, bound, slope, True), load_shares(amount, rows * top, bound, slope, False)
    places = jnp.arange(amount)

    def named(tallies, turn):
        used = int((tallies > 0).sum())
        fixed = max(1, used // 4)
        shifted = fixed + (places - fixed + turn * (used - fixed)) % max(1, amount - fixed)
        return jnp.zeros((amount,), jnp.int32).at[order[jnp.where(places < fixed, places, shifted)]].set(jnp.asarray(tallies, jnp.int32))

    tallies = jnp.where(number % 4 == 0, named(heavy_load, number // 4), named(usual, number - number // 4 - 1))
    mixed = jax.random.permutation(jax.random.fold_in(own, 3), amount)
    donor, receiver = mixed[0:amount // 2 * 2:2], mixed[1:amount // 2 * 2:2]
    slack = jnp.minimum(tallies[donor] - 1, bound - tallies[receiver]) // 2
    slack = jnp.where((donor == order[0]) | (receiver == order[0]) | (tallies[receiver] == 0), 0, jnp.maximum(slack, 0))
    shifted = jax.random.randint(jax.random.fold_in(own, 4), (amount // 2,), 0, 1 << 20) % (slack + 1)
    tallies = tallies.at[donor].add(-shifted).at[receiver].add(shifted)
    labels = jnp.searchsorted(jnp.cumsum(tallies), jnp.arange(rows * top), side="right").astype(jnp.int32)
    table = labels.reshape(top, rows).T
    table = table[jax.random.permutation(jax.random.fold_in(own, 1), rows)]
    turn = jax.random.randint(jax.random.fold_in(own, 2), (rows, 1), 0, top)
    return jnp.take_along_axis(table, (jnp.arange(top)[None, :] + turn) % top, axis=1)


def load_shares(number_of, total, bound, skew, full):
    portions = [(1 << 20) // math.isqrt(grade ** skew) + 1 for grade in range(1, number_of + 1)]
    largest = bound if full else min(bound, max(-(-total // number_of), total * portions[0] // sum(portions)))
    least = 1 if total - largest >= number_of - 1 else 0
    holding, surplus = [largest] + [least] * (number_of - 1), total - largest - least * (number_of - 1)
    while surplus > 0:
        free = [i for i in range(1, number_of) if holding[i] < largest] or [i for i in range(1, number_of) if holding[i] < bound]
        whole, budget = sum([portions[i] for i in free]), surplus
        for i in free:
            more = min(bound - holding[i], max(1, budget * portions[i] // whole), surplus)
            holding[i] = holding[i] + more
            surplus = surplus - more
    return np.array(holding)


def centred(own_key, shape, width, reach, pieces=(), kind=jnp.bfloat16):
    values = width * jax.random.normal(own_key, shape, jnp.float32)
    if pieces:
        values = values * levels(own_key, shape, pieces, -0.22, 0.18)
    return jnp.clip(values, -reach, reach).astype(kind)


def setup_inputs(seed: int = 0) -> dict:
    streams_of = jax.random.split(jax.random.key(seed), 8)
    conc = jnp.clip(0.049804688 + 0.9501953 * jax.random.uniform(streams_of[0], (E, SL, NR, NC), jnp.float32) ** levels(streams_of[0], (E, SL, NR, NC), ((2, 8),), -0.2, 0.2), 0.049804688, 1.0).astype(jnp.bfloat16)
    spectra = centred(streams_of[1], (VIEWS, RAYS, CH), 0.5, 4.0, ((0, 4), (1, 8)))
    path_slab_keys = jax.random.split(jax.random.fold_in(streams_of[2], 1), VIEWS * RAYS // RAYS_DEV)
    path_slab_turns = jax.random.permutation(jax.random.fold_in(streams_of[2], 3), VIEWS * RAYS // RAYS_DEV)
    path_slab = jax.vmap(lambda own, number: routed_block(jax.random.fold_in(streams_of[2], 2), own, number, RAYS_DEV, N_SLAB, 1, CAP, 2))(path_slab_keys, path_slab_turns).reshape((VIEWS, RAYS, 1))
    line_offset = place_ends(jax.random.randint(streams_of[3], (VIEWS, RAYS), 0, SL * ROWS_DEV), jax.random.fold_in(streams_of[3], 1), 0, (SL * ROWS_DEV) - 1).astype(jnp.int32)
    profile = jnp.clip(jnp.exp(jax.random.uniform(streams_of[4], (E, CH), jnp.float32, math.log(0.01), math.log(0.3))), 0.01, 0.3)
    beam_absorb = jnp.clip(jnp.exp(jax.random.uniform(streams_of[5], (E,), jnp.float32, math.log(0.1), math.log(0.6))), 0.1, 0.6)
    line_absorb = draw_line_absorb(jax.random.fold_in(streams_of[7], 71), 0)
    return dict(conc=conc, spectra=spectra, path_slab=path_slab, line_offset=line_offset, profile=profile, beam_absorb=beam_absorb, line_absorb=line_absorb)


def before_sum(values, forward):
    zeros = jnp.zeros_like(values[..., :1])
    if forward:
        return jnp.concatenate([zeros, jnp.cumsum(values, axis=-1)[..., :-1]], axis=-1)
    flipped = jnp.flip(values, axis=-1)
    summed = jnp.concatenate([zeros, jnp.cumsum(flipped, axis=-1)[..., :-1]], axis=-1)
    return jnp.flip(summed, axis=-1)


def band_sum(values, upward, band_reach):
    row_count = values.shape[-2]
    padded = jnp.pad(values, [(0, 0)] * (values.ndim - 2) + [(band_reach, band_reach), (0, 0)])
    total = jnp.zeros_like(values)
    for offset in range(1, band_reach + 1):
        start = band_reach + offset if upward else band_reach - offset
        total = total + padded[..., start:start + row_count, :]
    return total


def reference(conc, spectra, path_slab, line_offset, profile, beam_absorb, line_absorb):
    highest = lax.Precision.HIGHEST
    by_slice = jnp.moveaxis(conc, 1, 0)

    def transmit(maps):
        mu_beam = jnp.einsum('e,erc->rc', beam_absorb, maps, precision=highest)
        mu_line = jnp.einsum('ef,frc->erc', line_absorb, maps, precision=highest)
        passing = []
        for view in range(VIEWS):
            beam_path = before_sum(mu_beam, view < 2) / NC
            line_path = band_sum(mu_line, view % 2 == 0, BAND)
            passing.append(jnp.exp(-beam_path[None] - line_path))
        return passing

    def forward_slice(maps_bf):
        maps = maps_bf.astype(jnp.float32)
        passing = transmit(maps)
        return jnp.stack([jnp.sum(maps * factor, axis=-1) / NC for factor in passing])

    fluor = lax.map(forward_slice, by_slice)
    slice_of = (line_offset // ROWS_DEV).astype(jnp.int32)
    row_of = (path_slab[:, :, 0] * ROWS_DEV + line_offset % ROWS_DEV).astype(jnp.int32)
    grads = []
    for view in range(VIEWS):
        table = jnp.transpose(fluor[:, view], (0, 2, 1))
        ray_fluor = table[slice_of[view], row_of[view]]
        residual = jnp.dot(ray_fluor, profile, precision=highest) - spectra[view].astype(jnp.float32)
        ray_grad = jnp.dot(residual, profile.T, precision=highest)
        summed = jax.ops.segment_sum(ray_grad, slice_of[view] * NR + row_of[view], num_segments=SL * NR)
        grads.append(jnp.transpose(summed.reshape(SL, NR, E), (0, 2, 1)))
    line_grad = jnp.stack(grads, axis=1)

    def backward_slice(inputs):
        maps_bf, grads_view = inputs
        maps = maps_bf.astype(jnp.float32)
        passing = transmit(maps)
        total = jnp.zeros_like(maps)
        for view in range(VIEWS):
            pulled = grads_view[view][:, :, None]
            weight = -pulled * maps * passing[view]
            back_beam = before_sum(jnp.sum(weight, axis=0), not (view < 2)) / NC
            back_line = jnp.einsum('ef,erc->frc', line_absorb, band_sum(weight, view % 2 != 0, BAND), precision=highest)
            total = total + pulled * passing[view] + beam_absorb[:, None, None] * back_beam[None] + back_line
        return total

    result = lax.map(backward_slice, (by_slice, line_grad))
    return jnp.moveaxis(result, 0, 1)
```

```python
import functools

import jax
import jax.numpy as jnp
from jax import lax
from jax.experimental import pallas as pl
from jax.experimental.pallas import tpu as pltpu
from jax.sharding import PartitionSpec as P

f32, bf16, i32 = jnp.float32, jnp.bfloat16, jnp.int32
highest = lax.Precision.HIGHEST
MESH = pl.DeviceIdType.MESH

E, S, R, H = 8, 2, 16, 8
OWN, HALO = E * R, E * H
SIDE = OWN + HALO
LINES = 2 * SIDE


def iota(shape, dim):
    return lax.broadcasted_iota(i32, shape, dim)


def split(x):
    hi = x.astype(bf16)
    return hi, (x - hi.astype(f32)).astype(bf16)


def dot(a, b, precision=None):
    return jnp.dot(a, b, precision=precision, preferred_element_type=f32)


def side_index(index):
    own = index < OWN
    rest = index - OWN
    high = index >= SIDE
    element = jnp.where(own, index // R, (rest % HALO) // H)
    row = jnp.where(own, index % R, jnp.where(high, R, -H) + index % H)
    return element, row


def line_index(index):
    odd = index >= SIDE
    local = jnp.where(odd, index - SIDE, index)
    own = local < OWN
    element = jnp.where(own, local // R, (local - OWN) // H)
    row = jnp.where(own, local % R, jnp.where(odd, R, -H) + local % H)
    return odd, element, row


def kernel(slabs, views, cells, conc_ref, spectra_ref, dest_ref, offset_ref, profile_ref, beam_ref, absorb_ref,
           out_ref, own, low, high, low_out, high_out, fwd_hi, fwd_lo, back_hi, back_lo, tri, gram,
           passing, beams, weights, ray_send, ray_recv, tab, part, column, load_sem,
           halo_send_sem, halo_recv_sem, ray_send_sem, ray_recv_sem, tab_send_sem, tab_recv_sem,
           part_send_sem, part_recv_sem):
    me, block = lax.axis_index("slab"), lax.axis_index("ang")
    width = cells // views
    scale = 1.0 / cells

    loads = []
    for s in range(S):
        copy = pltpu.make_async_copy(
            conc_ref.at[:, s, :, pl.ds(pl.multiple_of(block * width, 128), width)], own.at[s], load_sem.at[s])
        copy.start()
        loads.append(copy)

    barrier = pltpu.get_barrier_semaphore()

    def greet(k, carry):
        pl.semaphore_signal(barrier, inc=1, device_id={"slab": lax.rem(me + k, slabs), "ang": block}, device_id_type=MESH)
        return carry

    lax.fori_loop(1, slabs, greet, 0)
    for k in range(1, views):
        pl.semaphore_signal(barrier, inc=1, device_id={"slab": me, "ang": lax.rem(block + k, views)}, device_id_type=MESH)

    @pl.when(me == 0)
    def _():
        low[...] = jnp.zeros_like(low)

    @pl.when(me == slabs - 1)
    def _():
        high[...] = jnp.zeros_like(high)

    for s in range(S):
        loads[s].wait()
        for i in range(E // 2):
            first = own[s, 2 * i].astype(f32)
            second = own[s, 2 * i + 1].astype(f32)
            low_out[s, i] = jnp.concatenate([first[:H], second[:H]], axis=0).astype(bf16)
            high_out[s, i] = jnp.concatenate([first[H:], second[H:]], axis=0).astype(bf16)

    pl.semaphore_wait(barrier, slabs - 1 + views - 1)

    def halo(s, upward):
        if upward:
            src, dst, target = high_out, low, me + 1
        else:
            src, dst, target = low_out, high, me - 1
        return pltpu.make_async_remote_copy(
            src_ref=src.at[s], dst_ref=dst.at[s],
            send_sem=halo_send_sem.at[int(upward), s], recv_sem=halo_recv_sem.at[int(upward), s],
            device_id={"slab": target, "ang": block}, device_id_type=MESH)

    for s in range(S):
        @pl.when(me < slabs - 1)
        def _():
            halo(s, True).start()

        @pl.when(me > 0)
        def _():
            halo(s, False).start()

    lanes = iota((1, 2 * OWN), 1)
    lane_element, _ = side_index(lanes)
    spread = (iota((E, 2 * OWN), 0) == lane_element).astype(f32)
    profile = profile_ref[...]
    expanded = lax.dot_general(spectra_ref[0].astype(f32), profile, (((1,), (1,)), ((), ())),
                               precision=highest, preferred_element_type=f32)
    rays = expanded.shape[0]
    expanded = dot(expanded, spread, highest)
    offsets = offset_ref[...]
    diagonal = iota((rays, rays), 0) == iota((rays, rays), 1)
    offset_col = jnp.sum(jnp.where(diagonal, offsets.astype(f32), 0.0), axis=1, keepdims=True).astype(i32)
    dest_col = jnp.sum(jnp.where(diagonal, dest_ref[...].astype(f32), 0.0), axis=1, keepdims=True).astype(i32)
    ray_row = dest_col * R + offset_col % R
    odd_view = block % 2
    halo_row = jnp.where(odd_view == 1, R, -H) + lanes % H
    lane_row = jnp.where(lanes < OWN, lanes % R, jnp.where(lanes < SIDE, halo_row, -(1 << 24)))
    row8 = iota((8, rays), 0)
    slice_hot = offsets // R == row8
    pick_sum = jnp.where(slice_hot & (row8 < S), 1.0, 0.0)
    pick_count = jnp.where((offsets // R == row8 - S) & (row8 >= S), 1.0, 0.0)

    def message(target):
        hit = (ray_row - target * R) == lane_row
        return dot(pick_sum, jnp.where(hit, expanded, 0.0), highest) + dot(
            pick_count.astype(bf16), jnp.where(hit, 1.0, 0.0).astype(bf16))

    def ray_copy(k):
        return pltpu.make_async_remote_copy(
            src_ref=ray_send.at[k], dst_ref=ray_recv.at[k], send_sem=ray_send_sem.at[k], recv_sem=ray_recv_sem.at[k],
            device_id={"slab": lax.rem(me + k, slabs), "ang": block}, device_id_type=MESH)

    def send_rays(k, carry):
        ray_send[k] = message(lax.rem(me + k, slabs))
        ray_copy(k).start()
        return carry

    lax.fori_loop(1, slabs, send_rays, 0)
    mine = message(me)

    m_index = iota((LINES, 1), 0)
    odd, m_element, m_row = line_index(m_index)
    k_index = iota((1, 2 * OWN), 1)
    k_element, k_row = side_index(k_index)
    ahead = jnp.where(odd, m_row - k_row, k_row - m_row)
    band = (ahead >= 1) & (ahead <= H)
    rows_hot = (m_element == iota((LINES, E), 1)).astype(bf16)
    cols_hot = spread.astype(bf16)
    absorb = absorb_ref[...]
    for piece, ref in zip(split(absorb), (fwd_hi, fwd_lo)):
        mixed = dot(dot(rows_hot, piece).astype(bf16), cols_hot)
        ref[:LINES] = jnp.where(band, mixed, 0.0).astype(bf16)
    b_row = jnp.zeros((1, 2 * OWN), f32)
    for e in range(E):
        b_row = jnp.where(k_element == e, beam_ref[e], b_row)
    beam_rows = iota((2 * R, 1), 0)
    beam_row = jnp.where(beam_rows < R, beam_rows, jnp.where(beam_rows < R + H, beam_rows - R - H, beam_rows - H))
    beam_mat = jnp.where(beam_row == k_row, b_row, 0.0)
    fwd_hi[LINES:], fwd_lo[LINES:] = split(beam_mat)

    n_index = iota((1, LINES), 1)
    n_odd, n_element, n_row = line_index(n_index)
    o_index = iota((OWN, 1), 0)
    o_element, o_row = o_index // R, o_index % R
    ahead = jnp.where(n_odd, n_row - o_row, o_row - n_row)
    band = (ahead >= 1) & (ahead <= H)
    rows_hot = (o_element == iota((OWN, E), 1)).astype(bf16)
    cols_hot = (iota((E, LINES), 0) == n_element).astype(bf16)
    for piece, ref in zip(split(absorb), (back_hi, back_lo)):
        left = lax.dot_general(rows_hot, piece, (((1,), (1,)), ((), ())), preferred_element_type=f32)
        ref[...] = jnp.where(band, dot(left.astype(bf16), cols_hot), 0.0).astype(bf16)

    tri[...] = jnp.where(iota((width, width), 0) < iota((width, width), 1), 1.0, 0.0).astype(bf16)

    small = lax.dot_general(profile, profile, (((1,), (1,)), ((), ())), precision=highest, preferred_element_type=f32)
    g_rows = iota((2 * OWN, 1), 0)
    g_element, g_row = side_index(g_rows)
    g_hot = (g_element == iota((2 * OWN, E), 1)).astype(f32)
    wide = dot(dot(g_hot, small, highest), spread, highest)
    gram[...] = jnp.where(g_row == k_row, wide, 0.0)


    def gather_rays(k, total):
        ray_copy(k).wait()
        return total + ray_recv[k]

    tab[0] = lax.fori_loop(1, slabs, gather_rays, mine)

    def to_view(ref, k, send, recv):
        return pltpu.make_async_remote_copy(
            src_ref=ref.at[0], dst_ref=ref.at[k], send_sem=send.at[k], recv_sem=recv.at[k],
            device_id={"slab": me, "ang": lax.rem(block + k, views)}, device_id_type=MESH)

    for k in range(1, views):
        to_view(tab, k, tab_send_sem, tab_recv_sem).start()

    lane = iota((1, 128), 1)
    column[...] = jnp.zeros_like(column)
    for s in range(S):
        @pl.when(me > 0)
        def _():
            halo(s, True).wait_recv()

        @pl.when(me < slabs - 1)
        def _():
            halo(s, False).wait_recv()

        maps = jnp.concatenate([own[s], low[s], high[s]], axis=0).reshape(2 * OWN, width)
        paths = dot(fwd_hi[...], maps) + dot(fwd_lo[...], maps)
        passing[s] = jnp.exp(-paths[:LINES])
        mu = paths[LINES:]
        mu_hi, mu_lo = split(mu)
        before = dot(mu_hi, tri[...]) + dot(mu_lo, tri[...])
        total = jnp.sum(mu, axis=1, keepdims=True)
        beams[s, 0] = jnp.exp(-scale * before)
        beams[s, 1] = jnp.exp(-scale * (total - before - mu))

        def put(rows, values, sums):
            merged = column[rows, :]
            for odd_side in range(2):
                for back in range(2):
                    k = 2 * (2 * back + odd_side) + s
                    flux = jnp.sum(values[odd_side][back], axis=1, keepdims=True)
                    merged = jnp.where(lane == k, flux, merged)
                    merged = jnp.where(lane == 8 + k, sums[odd_side], merged)
            column[rows, :] = merged

        for e in range(E):
            amount = own[s, e].astype(f32)
            values = []
            for odd_side in range(2):
                lit = amount * passing[s, odd_side * SIDE + e * R:odd_side * SIDE + (e + 1) * R]
                values.append([lit * beams[s, back, :R] for back in range(2)])
            put(slice(e * R, (e + 1) * R), values, (total[:R], total[:R]))
        for i in range(E // 2):
            values = []
            both = []
            for odd_side, ref in ((0, low), (1, high)):
                start = odd_side * SIDE + OWN + i * 2 * H
                lit = ref[s, i].astype(f32) * passing[s, start:start + 2 * H]
                rows = slice(R + odd_side * H, R + (odd_side + 1) * H)
                values.append([lit * jnp.concatenate([beams[s, back, rows]] * 2, axis=0) for back in range(2)])
                both.append(jnp.concatenate([total[rows]] * 2, axis=0))
            put(slice(OWN + i * 2 * H, OWN + (i + 1) * 2 * H), values, both)

    part[0] = jnp.transpose(column[...])[:16]
    for k in range(1, views):
        to_view(part, k, part_send_sem, part_recv_sem).start()
    for k in range(1, views):
        to_view(tab, k, tab_send_sem, tab_recv_sem).wait()

    row8 = iota((8, 1), 0)
    sums = jnp.zeros((8, 2 * OWN), f32)
    counts = jnp.zeros((8, 2 * OWN), f32)
    owner = [lax.rem(block + views - k, views) for k in range(views)]
    for k in range(views):
        for s in range(S):
            here = row8 == 2 * owner[k] + s
            sums = jnp.where(here, tab[k, s:s + 1, :], sums)
            counts = jnp.where(here, tab[k, S + s:S + s + 1, :], counts)

    for k in range(1, views):
        to_view(part, k, part_send_sem, part_recv_sem).wait()

    ahead_rows = row8 < 4
    blocks, scales = [], []
    for k in range(views):
        offset = jnp.zeros((8, 2 * OWN), f32)
        for j in range(views):
            if j != k:
                counted = (ahead_rows & (owner[j] < owner[k])) | (~ahead_rows & (owner[j] > owner[k]))
                offset = offset + jnp.where(counted, part[j, 8:16, :], 0.0)
        factor = jnp.exp(-scale * offset)
        scales.append(factor)
        blocks.append(part[k, 0:8, :] * factor)
    fluor = (blocks[0] + blocks[1] + blocks[2] + blocks[3]) * scale
    pulled = counts * dot(fluor, gram[...], highest) - sums
    later = jnp.zeros((8, 2 * OWN), f32)
    for k in range(views):
        counted = (ahead_rows & (owner[k] >= block)) | (~ahead_rows & (owner[k] < block))
        later = later + jnp.where(counted, blocks[k], 0.0)
    pad = jnp.zeros((112, 2 * OWN), f32)
    stacked = jnp.concatenate([pulled * scales[0], -pulled * later, pad], axis=0)
    column[...] = jnp.transpose(stacked)

    carry = column[0:R, :]
    for e in range(1, E):
        carry = carry + column[e * R:(e + 1) * R, :]

    for s in range(S):
        beam = [beams[s, 0, :R], beams[s, 1, :R]]
        seen = [jnp.zeros((R, width), f32), jnp.zeros((R, width), f32)]
        for e in range(E):
            amount = own[s, e].astype(f32)
            cols = column[e * R:(e + 1) * R, :]
            direct = None
            for odd_side in range(2):
                start = odd_side * SIDE + e * R
                through = passing[s, start:start + R]
                ahead_pull = cols[:, 2 * odd_side + s:2 * odd_side + s + 1]
                back_pull = cols[:, 4 + 2 * odd_side + s:4 + 2 * odd_side + s + 1]
                term = through * (ahead_pull * beam[0] + back_pull * beam[1])
                lit = amount * through
                seen[0] = seen[0] + lit * ahead_pull
                seen[1] = seen[1] + lit * back_pull
                weights[0, start:start + R], weights[1, start:start + R] = split(amount * term)
                direct = term if direct is None else direct + term
            out_ref[e, s] = direct
        for i in range(E // 2):
            cols = column[OWN + i * 2 * H:OWN + (i + 1) * 2 * H, :]
            for odd_side, ref in ((0, low), (1, high)):
                start = odd_side * SIDE + OWN + i * 2 * H
                rows = slice(R + odd_side * H, R + (odd_side + 1) * H)
                beam_h = [jnp.concatenate([beams[s, back, rows]] * 2, axis=0) for back in range(2)]
                ahead_pull = cols[:, 2 * odd_side + s:2 * odd_side + s + 1]
                back_pull = cols[:, 4 + 2 * odd_side + s:4 + 2 * odd_side + s + 1]
                term = passing[s, start:start + 2 * H] * (ahead_pull * beam_h[0] + back_pull * beam_h[1])
                weights[0, start:start + 2 * H], weights[1, start:start + 2 * H] = split(ref[s, i].astype(f32) * term)
        lines = dot(back_hi[...], weights[0]) + dot(back_lo[...], weights[0]) + dot(back_hi[...], weights[1])
        ahead_sum = beam[0] * seen[0]
        back_sum = beam[1] * seen[1]
        diff_hi, diff_lo = split(ahead_sum - back_sum)
        chosen = (lane >= 8) & (lane < 16) & (lane % 2 == s)
        extra = jnp.sum(jnp.where(chosen, carry, 0.0), axis=1, keepdims=True)
        back_beam = scale * (dot(diff_hi, tri[...]) + dot(diff_lo, tri[...]) + ahead_sum + extra)
        for e in range(E):
            out_ref[e, s] = out_ref[e, s] + beam_ref[e] * back_beam - lines[e * R:(e + 1) * R]

    for s in range(S):
        @pl.when(me < slabs - 1)
        def _():
            halo(s, True).wait_send()

        @pl.when(me > 0)
        def _():
            halo(s, False).wait_send()


def local(slabs, views, conc, spectra, path_slab, line_offset, profile, beam_absorb, line_absorb):
    cells = conc.shape[-1]
    width = cells // views
    vmem, smem = pl.BlockSpec(memory_space=pltpu.VMEM), pl.BlockSpec(memory_space=pltpu.SMEM)
    dma = pltpu.SemaphoreType.DMA
    return pl.pallas_call(
        functools.partial(kernel, slabs, views, cells),
        out_shape=jax.ShapeDtypeStruct((E, S, R, width), f32),
        in_specs=[pl.BlockSpec(memory_space=pl.ANY), vmem, vmem, vmem, vmem, smem, vmem],
        out_specs=vmem,
        scratch_shapes=[
            pltpu.VMEM((S, E, R, width), bf16),
            pltpu.VMEM((S, E // 2, 2 * H, width), bf16),
            pltpu.VMEM((S, E // 2, 2 * H, width), bf16),
            pltpu.VMEM((S, E // 2, 2 * H, width), bf16),
            pltpu.VMEM((S, E // 2, 2 * H, width), bf16),
            pltpu.VMEM((LINES + 2 * R, 2 * OWN), bf16),
            pltpu.VMEM((LINES + 2 * R, 2 * OWN), bf16),
            pltpu.VMEM((OWN, LINES), bf16),
            pltpu.VMEM((OWN, LINES), bf16),
            pltpu.VMEM((width, width), bf16),
            pltpu.VMEM((2 * OWN, 2 * OWN), f32),
            pltpu.VMEM((S, LINES, width), f32),
            pltpu.VMEM((S, 2, 2 * R, width), f32),
            pltpu.VMEM((2, LINES, width), bf16),
            pltpu.VMEM((slabs, 8, 2 * OWN), f32),
            pltpu.VMEM((slabs, 8, 2 * OWN), f32),
            pltpu.VMEM((views, 8, 2 * OWN), f32),
            pltpu.VMEM((views, 16, 2 * OWN), f32),
            pltpu.VMEM((2 * OWN, 128), f32),
            dma((S,)),
            dma((2, S)),
            dma((2, S)),
            dma((slabs,)),
            dma((slabs,)),
            dma((views,)),
            dma((views,)),
            dma((views,)),
            dma((views,)),
        ],
        compiler_params=pltpu.CompilerParams(
            collective_id=0, has_side_effects=True, vmem_limit_bytes=40 * 1024 * 1024),
    )(conc, spectra, path_slab.reshape(1, -1), line_offset, profile, beam_absorb, line_absorb)


def solution(mesh):
    slabs, views = mesh.shape["slab"], mesh.shape["ang"]
    in_specs = (
        P(None, None, "slab", None),
        P("ang", "slab", None),
        P("ang", "slab", None),
        P("ang", "slab"),
        P(),
        P(),
        P(),
    )
    out_specs = P(None, None, "slab", "ang")
    return jax.shard_map(functools.partial(local, slabs, views), mesh=mesh, in_specs=in_specs, out_specs=out_specs,
                         check_vma=False)
```

```python
import functools

import jax
import jax.numpy as jnp
from jax import lax
from jax.experimental import pallas as pl
from jax.experimental.pallas import tpu as pltpu
from jax.sharding import PartitionSpec as P

f32, bf16, i32 = jnp.float32, jnp.bfloat16, jnp.int32
highest = lax.Precision.HIGHEST
MESH = pl.DeviceIdType.MESH

E, S, R, H = 8, 2, 16, 8
OWN, HALO = E * R, E * H
SIDE = OWN + HALO
LINES = 2 * SIDE


def iota(shape, dim):
    return lax.broadcasted_iota(i32, shape, dim)


def split(x):
    hi = x.astype(bf16)
    return hi, (x - hi.astype(f32)).astype(bf16)


def dot(a, b, precision=None):
    return jnp.dot(a, b, precision=precision, preferred_element_type=f32)


def side_index(index):
    own = index < OWN
    rest = index - OWN
    high = index >= SIDE
    element = jnp.where(own, index >> 4, (rest & (HALO - 1)) >> 3)
    row = jnp.where(own, index & (R - 1), jnp.where(high, R, -H) + (index & (H - 1)))
    return element, row


def line_index(index):
    odd = index >= SIDE
    local = jnp.where(odd, index - SIDE, index)
    own = local < OWN
    element = jnp.where(own, local >> 4, (local - OWN) >> 3)
    row = jnp.where(own, local & (R - 1), jnp.where(odd, R, -H) + (local & (H - 1)))
    return odd, element, row


def kernel(slabs, views, cells, conc_ref, *refs):
    small_in, out_ref, small_refs, rest = refs[:6], refs[6], refs[7:13], refs[13:]
    spectra_ref, dest_ref, offset_ref, profile_ref, beam_ref, absorb_ref = small_refs
    (own, low, high, low_out, high_out, fwd_hi, fwd_lo, back_hi, back_lo, tri, gram_hi, gram_lo,
     passing, beams, weights, ray_send, ray_recv, tab, part, column, load_sem, small_sem,
     halo_send_sem, halo_recv_sem, ray_send_sem, ray_recv_sem, tab_send_sem, tab_recv_sem,
     part_send_sem, part_recv_sem) = rest
    me, block = lax.axis_index("slab"), lax.axis_index("ang")
    width = cells // views
    scale = 1.0 / cells

    loads = []
    for s in range(S):
        copy = pltpu.make_async_copy(
            conc_ref.at[:, s, :, pl.ds(pl.multiple_of(block * width, 128), width)], own.at[s], load_sem.at[s])
        copy.start()
        loads.append(copy)
    small_loads = []
    for i in range(6):
        copy = pltpu.make_async_copy(small_in[i], small_refs[i], small_sem.at[i])
        copy.start()
        small_loads.append(copy)

    barrier = pltpu.get_barrier_semaphore()

    def greet(k, carry):
        pl.semaphore_signal(barrier, inc=1, device_id={"slab": lax.rem(me + k, slabs), "ang": block}, device_id_type=MESH)
        return carry

    lax.fori_loop(1, slabs, greet, 0)
    for k in range(1, views):
        pl.semaphore_signal(barrier, inc=1, device_id={"slab": me, "ang": lax.rem(block + k, views)}, device_id_type=MESH)

    @pl.when(me == 0)
    def _():
        low[...] = jnp.zeros_like(low)

    @pl.when(me == slabs - 1)
    def _():
        high[...] = jnp.zeros_like(high)

    for s in range(S):
        loads[s].wait()
        for i in range(E // 2):
            first = own[s, 2 * i].astype(f32)
            second = own[s, 2 * i + 1].astype(f32)
            low_out[s, i] = jnp.concatenate([first[:H], second[:H]], axis=0).astype(bf16)
            high_out[s, i] = jnp.concatenate([first[H:], second[H:]], axis=0).astype(bf16)

    pl.semaphore_wait(barrier, slabs - 1 + views - 1)

    def halo(s, upward):
        if upward:
            src, dst, target = high_out, low, me + 1
        else:
            src, dst, target = low_out, high, me - 1
        return pltpu.make_async_remote_copy(
            src_ref=src.at[s], dst_ref=dst.at[s],
            send_sem=halo_send_sem.at[int(upward), s], recv_sem=halo_recv_sem.at[int(upward), s],
            device_id={"slab": target, "ang": block}, device_id_type=MESH)

    for s in range(S):
        @pl.when(me < slabs - 1)
        def _():
            halo(s, True).start()

        @pl.when(me > 0)
        def _():
            halo(s, False).start()

    for copy in small_loads:
        copy.wait()
    lanes = iota((1, 2 * OWN), 1)
    lane_element, _ = side_index(lanes)
    spread = (iota((E, 2 * OWN), 0) == lane_element).astype(f32)
    profile = profile_ref[...]
    flat = (((1,), (1,)), ((), ()))
    lines_of = sum(lax.dot_general(spectra_ref[0], piece, flat, preferred_element_type=f32) for piece in split(profile))
    rays = lines_of.shape[0]
    expanded = [dot(piece, spread.astype(bf16)) for piece in split(lines_of)]
    offsets = offset_ref[...]
    diagonal = iota((rays, rays), 0) == iota((rays, rays), 1)
    ray_row = (dest_ref[...] << 4) + (offsets & (R - 1))
    ray_row = jnp.sum(jnp.where(diagonal, ray_row, 0).astype(f32), axis=1, keepdims=True).astype(i32)
    odd_view = block % 2
    halo_row = jnp.where(odd_view == 1, R, -H) + (lanes & (H - 1))
    lane_row = jnp.where(lanes < OWN, lanes & (R - 1), jnp.where(lanes < SIDE, halo_row, -(1 << 24)))
    ray_gap = ray_row - lane_row
    row8 = iota((8, rays), 0)
    ray_slice = offsets >> 4
    pick_sum = jnp.where(ray_slice == row8, 1.0, 0.0)
    pick_count = jnp.where(ray_slice == row8 - S, 1.0, 0.0)
    pick = jnp.concatenate([pick_sum, pick_sum, pick_count, jnp.zeros_like(pick_sum)], axis=1).astype(bf16)

    def message(target):
        hit = ray_gap == target * R
        picked = [jnp.where(hit, x, 0.0) for x in (*expanded, 1.0)]
        return dot(pick, jnp.concatenate(picked + [jnp.zeros_like(picked[0])], axis=0).astype(bf16))

    def ray_copy(k):
        return pltpu.make_async_remote_copy(
            src_ref=ray_send.at[k], dst_ref=ray_recv.at[k], send_sem=ray_send_sem.at[k], recv_sem=ray_recv_sem.at[k],
            device_id={"slab": lax.rem(me + k, slabs), "ang": block}, device_id_type=MESH)

    def send_rays(k, carry):
        ray_send[k] = message(lax.rem(me + k, slabs))
        ray_copy(k).start()
        return carry

    lax.fori_loop(1, slabs, send_rays, 0)
    mine = message(me)

    m_index = iota((LINES, 1), 0)
    odd, m_element, m_row = line_index(m_index)
    k_index = iota((1, 2 * OWN), 1)
    k_element, k_row = side_index(k_index)
    ahead = jnp.where(odd, m_row - k_row, k_row - m_row)
    band = (ahead >= 1) & (ahead <= H)
    rows_hot = (m_element == iota((LINES, E), 1)).astype(bf16)
    cols_hot = spread.astype(bf16)
    absorb = absorb_ref[...]
    for piece, ref in zip(split(absorb), (fwd_hi, fwd_lo)):
        mixed = dot(dot(rows_hot, piece).astype(bf16), cols_hot)
        ref[:LINES] = jnp.where(band, mixed, 0.0).astype(bf16)
    b_row = jnp.zeros((1, 2 * OWN), f32)
    for e in range(E):
        b_row = jnp.where(k_element == e, beam_ref[e], b_row)
    beam_rows = iota((2 * R, 1), 0)
    beam_row = jnp.where(beam_rows < R, beam_rows, jnp.where(beam_rows < R + H, beam_rows - R - H, beam_rows - H))
    beam_mat = jnp.where(beam_row == k_row, b_row, 0.0)
    fwd_hi[LINES:], fwd_lo[LINES:] = split(beam_mat)

    n_index = iota((1, LINES), 1)
    n_odd, n_element, n_row = line_index(n_index)
    o_index = iota((OWN, 1), 0)
    o_element, o_row = o_index >> 4, o_index & (R - 1)
    ahead = jnp.where(n_odd, n_row - o_row, o_row - n_row)
    band = (ahead >= 1) & (ahead <= H)
    rows_hot = (o_element == iota((OWN, E), 1)).astype(bf16)
    cols_hot = (iota((E, LINES), 0) == n_element).astype(bf16)
    for piece, ref in zip(split(absorb), (back_hi, back_lo)):
        left = lax.dot_general(rows_hot, piece, (((1,), (1,)), ((), ())), preferred_element_type=f32)
        ref[...] = jnp.where(band, dot(left.astype(bf16), cols_hot), 0.0).astype(bf16)

    tri[...] = jnp.where(iota((width, width), 0) < iota((width, width), 1), 1.0, 0.0).astype(bf16)

    small = lax.dot_general(profile, profile, flat, precision=highest, preferred_element_type=f32)
    g_rows = iota((2 * OWN, 1), 0)
    g_element, g_row = side_index(g_rows)
    g_hot = (g_element == iota((2 * OWN, E), 1)).astype(bf16)
    for piece, ref in zip(split(small), (gram_hi, gram_lo)):
        wide = dot(dot(g_hot, piece).astype(bf16), spread.astype(bf16))
        ref[...] = jnp.where(g_row == k_row, wide, 0.0).astype(bf16)

    lane = iota((1, 128), 1)
    column[...] = jnp.zeros_like(column)
    for s in range(S):
        @pl.when(me > 0)
        def _():
            halo(s, True).wait_recv()

        @pl.when(me < slabs - 1)
        def _():
            halo(s, False).wait_recv()

        maps = jnp.concatenate([own[s], low[s], high[s]], axis=0).reshape(2 * OWN, width)
        paths = dot(fwd_hi[...], maps) + dot(fwd_lo[...], maps)
        passing[s] = jnp.exp(-paths[:LINES])
        mu = paths[LINES:]
        mu_hi, mu_lo = split(mu)
        before = dot(mu_hi, tri[...]) + dot(mu_lo, tri[...])
        total = jnp.sum(mu, axis=1, keepdims=True)
        beams[s, 0] = jnp.exp(-scale * before)
        beams[s, 1] = jnp.exp(-scale * (total - before - mu))

        def put(rows, values, sums):
            merged = column[rows, :]
            for odd_side in range(2):
                for back in range(2):
                    k = 2 * (2 * back + odd_side) + s
                    flux = jnp.sum(values[odd_side][back], axis=1, keepdims=True)
                    merged = jnp.where(lane == k, flux, merged)
                    merged = jnp.where(lane == 8 + k, sums[odd_side], merged)
            column[rows, :] = merged

        for e in range(E):
            amount = own[s, e].astype(f32)
            values = []
            for odd_side in range(2):
                lit = amount * passing[s, odd_side * SIDE + e * R:odd_side * SIDE + (e + 1) * R]
                values.append([lit * beams[s, back, :R] for back in range(2)])
            put(slice(e * R, (e + 1) * R), values, (total[:R], total[:R]))
        for i in range(E // 2):
            values = []
            both = []
            for odd_side, ref in ((0, low), (1, high)):
                start = odd_side * SIDE + OWN + i * 2 * H
                lit = ref[s, i].astype(f32) * passing[s, start:start + 2 * H]
                rows = slice(R + odd_side * H, R + (odd_side + 1) * H)
                values.append([lit * jnp.concatenate([beams[s, back, rows]] * 2, axis=0) for back in range(2)])
                both.append(jnp.concatenate([total[rows]] * 2, axis=0))
            put(slice(OWN + i * 2 * H, OWN + (i + 1) * 2 * H), values, both)


    def gather_rays(k, total):
        ray_copy(k).wait()
        return total + ray_recv[k]

    def to_view(ref, k, send, recv):
        return pltpu.make_async_remote_copy(
            src_ref=ref.at[0], dst_ref=ref.at[k], send_sem=send.at[k], recv_sem=recv.at[k],
            device_id={"slab": me, "ang": lax.rem(block + k, views)}, device_id_type=MESH)

    part[0] = jnp.transpose(column[...])[:16]
    for k in range(1, views):
        to_view(part, k, part_send_sem, part_recv_sem).start()
    tab[0] = lax.fori_loop(1, slabs, gather_rays, mine)
    for k in range(1, views):
        to_view(tab, k, tab_send_sem, tab_recv_sem).start()

    for k in range(1, views):
        to_view(tab, k, tab_send_sem, tab_recv_sem).wait()

    row8 = iota((8, 1), 0)
    sums = jnp.zeros((8, 2 * OWN), f32)
    counts = jnp.zeros((8, 2 * OWN), f32)
    owner = [lax.rem(block + views - k, views) for k in range(views)]
    for k in range(views):
        for s in range(S):
            here = row8 == 2 * owner[k] + s
            sums = jnp.where(here, tab[k, s:s + 1, :], sums)
            counts = jnp.where(here, tab[k, S + s:S + s + 1, :], counts)

    for k in range(1, views):
        to_view(part, k, part_send_sem, part_recv_sem).wait()

    ahead_rows = row8 < 4
    blocks, scales = [], []
    for k in range(views):
        offset = jnp.zeros((8, 2 * OWN), f32)
        for j in range(views):
            if j != k:
                counted = (ahead_rows & (owner[j] < owner[k])) | (~ahead_rows & (owner[j] > owner[k]))
                offset = offset + jnp.where(counted, part[j, 8:16, :], 0.0)
        factor = jnp.exp(-scale * offset)
        scales.append(factor)
        blocks.append(part[k, 0:8, :] * factor)
    fluor = (blocks[0] + blocks[1] + blocks[2] + blocks[3]) * scale
    fluor_hi, fluor_lo = split(fluor)
    mixed = dot(fluor_hi, gram_hi[...]) + dot(fluor_lo, gram_hi[...]) + dot(fluor_hi, gram_lo[...])
    pulled = counts * mixed - sums
    later = jnp.zeros((8, 2 * OWN), f32)
    for k in range(views):
        counted = (ahead_rows & (owner[k] >= block)) | (~ahead_rows & (owner[k] < block))
        later = later + jnp.where(counted, blocks[k], 0.0)
    pad = jnp.zeros((112, 2 * OWN), f32)
    stacked = jnp.concatenate([pulled * scales[0], -pulled * later, pad], axis=0)
    column[...] = jnp.transpose(stacked)

    carry = column[0:R, :]
    for e in range(1, E):
        carry = carry + column[e * R:(e + 1) * R, :]

    for s in range(S):
        beam = [beams[s, 0, :R], beams[s, 1, :R]]
        seen = [jnp.zeros((R, width), f32), jnp.zeros((R, width), f32)]
        for e in range(E):
            amount = own[s, e].astype(f32)
            cols = column[e * R:(e + 1) * R, :]
            direct = None
            for odd_side in range(2):
                start = odd_side * SIDE + e * R
                through = passing[s, start:start + R]
                ahead_pull = cols[:, 2 * odd_side + s:2 * odd_side + s + 1]
                back_pull = cols[:, 4 + 2 * odd_side + s:4 + 2 * odd_side + s + 1]
                term = through * (ahead_pull * beam[0] + back_pull * beam[1])
                lit = amount * through
                seen[0] = seen[0] + lit * ahead_pull
                seen[1] = seen[1] + lit * back_pull
                weights[0, start:start + R], weights[1, start:start + R] = split(amount * term)
                direct = term if direct is None else direct + term
            out_ref[e, s] = direct
        for i in range(E // 2):
            cols = column[OWN + i * 2 * H:OWN + (i + 1) * 2 * H, :]
            for odd_side, ref in ((0, low), (1, high)):
                start = odd_side * SIDE + OWN + i * 2 * H
                rows = slice(R + odd_side * H, R + (odd_side + 1) * H)
                beam_h = [jnp.concatenate([beams[s, back, rows]] * 2, axis=0) for back in range(2)]
                ahead_pull = cols[:, 2 * odd_side + s:2 * odd_side + s + 1]
                back_pull = cols[:, 4 + 2 * odd_side + s:4 + 2 * odd_side + s + 1]
                term = passing[s, start:start + 2 * H] * (ahead_pull * beam_h[0] + back_pull * beam_h[1])
                weights[0, start:start + 2 * H], weights[1, start:start + 2 * H] = split(ref[s, i].astype(f32) * term)
        lines = dot(back_hi[...], weights[0]) + dot(back_lo[...], weights[0]) + dot(back_hi[...], weights[1])
        ahead_sum = beam[0] * seen[0]
        back_sum = beam[1] * seen[1]
        diff_hi, diff_lo = split(ahead_sum - back_sum)
        chosen = (lane >= 8) & (lane < 16) & (lane % 2 == s)
        extra = jnp.sum(jnp.where(chosen, carry, 0.0), axis=1, keepdims=True)
        back_beam = scale * (dot(diff_hi, tri[...]) + dot(diff_lo, tri[...]) + ahead_sum + extra)
        for e in range(E):
            out_ref[e, s] = out_ref[e, s] + beam_ref[e] * back_beam - lines[e * R:(e + 1) * R]

    for s in range(S):
        @pl.when(me < slabs - 1)
        def _():
            halo(s, True).wait_send()

        @pl.when(me > 0)
        def _():
            halo(s, False).wait_send()


def local(slabs, views, conc, spectra, path_slab, line_offset, profile, beam_absorb, line_absorb):
    cells = conc.shape[-1]
    width = cells // views
    inputs = (conc, spectra, path_slab.reshape(1, -1), line_offset, profile, beam_absorb, line_absorb)
    dma = pltpu.SemaphoreType.DMA
    return pl.pallas_call(
        functools.partial(kernel, slabs, views, cells),
        out_shape=jax.ShapeDtypeStruct((E, S, R, width), f32),
        in_specs=[pl.BlockSpec(memory_space=pltpu.HBM)] * len(inputs),
        out_specs=pl.BlockSpec(memory_space=pltpu.VMEM),
        scratch_shapes=[
            pltpu.SMEM(x.shape, x.dtype) if x is beam_absorb else pltpu.VMEM(x.shape, x.dtype) for x in inputs[1:]
        ] + [
            pltpu.VMEM((S, E, R, width), bf16),
            pltpu.VMEM((S, E // 2, 2 * H, width), bf16),
            pltpu.VMEM((S, E // 2, 2 * H, width), bf16),
            pltpu.VMEM((S, E // 2, 2 * H, width), bf16),
            pltpu.VMEM((S, E // 2, 2 * H, width), bf16),
            pltpu.VMEM((LINES + 2 * R, 2 * OWN), bf16),
            pltpu.VMEM((LINES + 2 * R, 2 * OWN), bf16),
            pltpu.VMEM((OWN, LINES), bf16),
            pltpu.VMEM((OWN, LINES), bf16),
            pltpu.VMEM((width, width), bf16),
            pltpu.VMEM((2 * OWN, 2 * OWN), bf16),
            pltpu.VMEM((2 * OWN, 2 * OWN), bf16),
            pltpu.VMEM((S, LINES, width), f32),
            pltpu.VMEM((S, 2, 2 * R, width), f32),
            pltpu.VMEM((2, LINES, width), bf16),
            pltpu.VMEM((slabs, 8, 2 * OWN), f32),
            pltpu.VMEM((slabs, 8, 2 * OWN), f32),
            pltpu.VMEM((views, 8, 2 * OWN), f32),
            pltpu.VMEM((views, 16, 2 * OWN), f32),
            pltpu.VMEM((2 * OWN, 128), f32),
            dma((S,)),
            dma((len(inputs) - 1,)),
            dma((2, S)),
            dma((2, S)),
            dma((slabs,)),
            dma((slabs,)),
            dma((views,)),
            dma((views,)),
            dma((views,)),
            dma((views,)),
        ],
        compiler_params=pltpu.CompilerParams(
            collective_id=0, has_side_effects=True, vmem_limit_bytes=63 * 1024 * 1024),
    )(*inputs)


def solution(mesh):
    slabs, views = mesh.shape["slab"], mesh.shape["ang"]
    in_specs = (
        P(None, None, "slab", None),
        P("ang", "slab", None),
        P("ang", "slab", None),
        P("ang", "slab"),
        P(),
        P(),
        P(),
    )
    out_specs = P(None, None, "slab", "ang")
    return jax.shard_map(functools.partial(local, slabs, views), mesh=mesh, in_specs=in_specs, out_specs=out_specs,
                         check_vma=False)
```

```python
import functools

import jax
import jax.numpy as jnp
from jax import lax
from jax.experimental import pallas as pl
from jax.experimental.pallas import tpu as pltpu
from jax.sharding import PartitionSpec as P

f32, bf16, i32 = jnp.float32, jnp.bfloat16, jnp.int32
highest = lax.Precision.HIGHEST
MESH = pl.DeviceIdType.MESH

E, S, R, H = 8, 2, 16, 8
OWN, HALO = E * R, E * H
SIDE = OWN + HALO
LINES = 2 * SIDE


def iota(shape, dim):
    return lax.broadcasted_iota(i32, shape, dim)


def split(x):
    hi = x.astype(bf16)
    return hi, (x - hi.astype(f32)).astype(bf16)


def dot(a, b, precision=None):
    return jnp.dot(a, b, precision=precision, preferred_element_type=f32)


def side_index(index):
    own = index < OWN
    rest = index - OWN
    high = index >= SIDE
    element = jnp.where(own, index >> 4, (rest & (HALO - 1)) >> 3)
    row = jnp.where(own, index & (R - 1), jnp.where(high, R, -H) + (index & (H - 1)))
    return element, row


def line_index(index):
    odd = index >= SIDE
    local = jnp.where(odd, index - SIDE, index)
    own = local < OWN
    element = jnp.where(own, local >> 4, (local - OWN) >> 3)
    row = jnp.where(own, local & (R - 1), jnp.where(odd, R, -H) + (local & (H - 1)))
    return odd, element, row


def kernel(slabs, views, cells, conc_ref, *refs):
    small_in, out_ref, small_refs, rest = refs[:6], refs[6], refs[7:13], refs[13:]
    spectra_ref, dest_ref, offset_ref, profile_ref, beam_ref, absorb_ref = small_refs
    (own, low, high, low_out, high_out, fwd_hi, fwd_lo, back_hi, back_lo, tri, gram_hi, gram_lo,
     passing, beams, weights, ray_send, ray_recv, tab, part, column, stack, result, load_sem, small_sem, out_sem,
     halo_send_sem, halo_recv_sem, ray_send_sem, ray_recv_sem, tab_send_sem, tab_recv_sem,
     part_send_sem, part_recv_sem) = rest
    me, block = lax.axis_index("slab"), lax.axis_index("ang")
    width = cells // views
    scale = 1.0 / cells

    loads = []
    for s in range(S):
        copy = pltpu.make_async_copy(
            conc_ref.at[:, s, :, pl.ds(pl.multiple_of(block * width, 128), width)], own.at[s], load_sem.at[s])
        copy.start()
        loads.append(copy)
    small_loads = []
    for i in range(6):
        copy = pltpu.make_async_copy(small_in[i], small_refs[i], small_sem.at[i])
        copy.start()
        small_loads.append(copy)

    barrier = pltpu.get_barrier_semaphore()

    def greet(k, carry):
        pl.semaphore_signal(barrier, inc=1, device_id={"slab": lax.rem(me + k, slabs), "ang": block}, device_id_type=MESH)
        return carry

    lax.fori_loop(1, slabs, greet, 0)
    for k in range(1, views):
        pl.semaphore_signal(barrier, inc=1, device_id={"slab": me, "ang": lax.rem(block + k, views)}, device_id_type=MESH)

    @pl.when(me == 0)
    def _():
        low[...] = jnp.zeros_like(low)

    @pl.when(me == slabs - 1)
    def _():
        high[...] = jnp.zeros_like(high)

    def halo(s, upward):
        if upward:
            src, dst, target = high_out, low, me + 1
        else:
            src, dst, target = low_out, high, me - 1
        return pltpu.make_async_remote_copy(
            src_ref=src.at[s], dst_ref=dst.at[s],
            send_sem=halo_send_sem.at[int(upward), s], recv_sem=halo_recv_sem.at[int(upward), s],
            device_id={"slab": target, "ang": block}, device_id_type=MESH)

    for s in range(S):
        loads[s].wait()
        for i in range(E // 2):
            first = own[s, 2 * i].astype(f32)
            second = own[s, 2 * i + 1].astype(f32)
            low_out[s, i] = jnp.concatenate([first[:H], second[:H]], axis=0).astype(bf16)
            high_out[s, i] = jnp.concatenate([first[H:], second[H:]], axis=0).astype(bf16)
        if s == 0:
            pl.semaphore_wait(barrier, slabs - 1 + views - 1)

        @pl.when(me < slabs - 1)
        def _():
            halo(s, True).start()

        @pl.when(me > 0)
        def _():
            halo(s, False).start()

    for copy in small_loads:
        copy.wait()
    lanes = iota((1, 2 * OWN), 1)
    lane_element, _ = side_index(lanes)
    spread = (iota((E, 2 * OWN), 0) == lane_element).astype(f32)
    profile = profile_ref[...]
    flat = (((1,), (1,)), ((), ()))
    lines_of = sum(lax.dot_general(spectra_ref[0], piece, flat, preferred_element_type=f32) for piece in split(profile))
    rays = lines_of.shape[0]
    expanded = [dot(piece, spread.astype(bf16)) for piece in split(lines_of)]
    offsets = offset_ref[...]
    diagonal = iota((rays, rays), 0) == iota((rays, rays), 1)
    ray_row = (dest_ref[...] << 4) + (offsets & (R - 1))
    ray_row = jnp.sum(jnp.where(diagonal, ray_row, 0).astype(f32), axis=1, keepdims=True).astype(i32)
    odd_view = block % 2
    halo_row = jnp.where(odd_view == 1, R, -H) + (lanes & (H - 1))
    lane_row = jnp.where(lanes < OWN, lanes & (R - 1), jnp.where(lanes < SIDE, halo_row, -(1 << 24)))
    ray_gap = ray_row - lane_row
    row8 = iota((8, rays), 0)
    ray_slice = offsets >> 4
    pick_sum = jnp.where(ray_slice == row8, 1.0, 0.0)
    pick_count = jnp.where(ray_slice == row8 - S, 1.0, 0.0)
    pick = jnp.concatenate([pick_sum, pick_sum, pick_count, jnp.zeros_like(pick_sum)], axis=1).astype(bf16)

    def message(target):
        hit = ray_gap == target * R
        picked = [jnp.where(hit, x, 0.0) for x in (*expanded, 1.0)]
        return dot(pick, jnp.concatenate(picked + [jnp.zeros_like(picked[0])], axis=0).astype(bf16))

    def ray_copy(k):
        return pltpu.make_async_remote_copy(
            src_ref=ray_send.at[k], dst_ref=ray_recv.at[k], send_sem=ray_send_sem.at[k], recv_sem=ray_recv_sem.at[k],
            device_id={"slab": lax.rem(me + k, slabs), "ang": block}, device_id_type=MESH)

    def send_rays(k, carry):
        ray_send[k] = message(lax.rem(me + k, slabs))
        ray_copy(k).start()
        return carry

    lax.fori_loop(1, slabs, send_rays, 0)
    mine = message(me)

    m_index = iota((LINES, 1), 0)
    odd, m_element, m_row = line_index(m_index)
    k_index = iota((1, 2 * OWN), 1)
    k_element, k_row = side_index(k_index)
    ahead = jnp.where(odd, m_row - k_row, k_row - m_row)
    band = (ahead >= 1) & (ahead <= H)
    rows_hot = (m_element == iota((LINES, E), 1)).astype(bf16)
    cols_hot = spread.astype(bf16)
    absorb = absorb_ref[...]
    for piece, ref in zip(split(absorb), (fwd_hi, fwd_lo)):
        mixed = dot(dot(rows_hot, piece).astype(bf16), cols_hot)
        ref[:LINES] = jnp.where(band, mixed, 0.0).astype(bf16)
    b_row = jnp.zeros((1, 2 * OWN), f32)
    for e in range(E):
        b_row = jnp.where(k_element == e, beam_ref[e], b_row)
    beam_rows = iota((2 * R, 1), 0)
    beam_row = jnp.where(beam_rows < R, beam_rows, jnp.where(beam_rows < R + H, beam_rows - R - H, beam_rows - H))
    beam_mat = jnp.where(beam_row == k_row, b_row, 0.0)
    fwd_hi[LINES:], fwd_lo[LINES:] = split(beam_mat)

    n_index = iota((1, LINES), 1)
    n_odd, n_element, n_row = line_index(n_index)
    o_index = iota((OWN, 1), 0)
    o_element, o_row = o_index >> 4, o_index & (R - 1)
    ahead = jnp.where(n_odd, n_row - o_row, o_row - n_row)
    band = (ahead >= 1) & (ahead <= H)
    rows_hot = (o_element == iota((OWN, E), 1)).astype(bf16)
    cols_hot = (iota((E, LINES), 0) == n_element).astype(bf16)
    for piece, ref in zip(split(absorb), (back_hi, back_lo)):
        left = lax.dot_general(rows_hot, piece, (((1,), (1,)), ((), ())), preferred_element_type=f32)
        ref[...] = jnp.where(band, dot(left.astype(bf16), cols_hot), 0.0).astype(bf16)

    tri[...] = jnp.where(iota((width, width), 0) < iota((width, width), 1), 1.0, 0.0).astype(bf16)

    small = lax.dot_general(profile, profile, flat, precision=highest, preferred_element_type=f32)
    g_rows = iota((2 * OWN, 1), 0)
    g_element, g_row = side_index(g_rows)
    g_hot = (g_element == iota((2 * OWN, E), 1)).astype(bf16)
    for piece, ref in zip(split(small), (gram_hi, gram_lo)):
        wide = dot(dot(g_hot, piece).astype(bf16), spread.astype(bf16))
        ref[...] = jnp.where(g_row == k_row, wide, 0.0).astype(bf16)

    def gather_rays(k, total):
        ray_copy(k).wait()
        return total + ray_recv[k]

    def to_view(src, dst, k, send, recv):
        return pltpu.make_async_remote_copy(
            src_ref=src, dst_ref=dst, send_sem=send, recv_sem=recv,
            device_id={"slab": me, "ang": lax.rem(block + k, views)}, device_id_type=MESH)

    def tab_copy(k):
        return to_view(tab.at[0], tab.at[k], k, tab_send_sem.at[k], tab_recv_sem.at[k])

    def part_copy(s, k):
        return to_view(part.at[s, 0], part.at[s, k], k, part_send_sem.at[s, k], part_recv_sem.at[s, k])

    lane = iota((1, 128), 1)
    column[:, SIDE:, :] = jnp.zeros((S, 2 * OWN - SIDE, 128), f32)
    for s in range(S):
        @pl.when(me > 0)
        def _():
            halo(s, True).wait_recv()

        @pl.when(me < slabs - 1)
        def _():
            halo(s, False).wait_recv()

        if s == S - 1:
            tab[0] = lax.fori_loop(1, slabs, gather_rays, mine)
            for k in range(1, views):
                tab_copy(k).start()

        maps = jnp.concatenate([own[s], low[s], high[s]], axis=0).reshape(2 * OWN, width)
        paths = dot(fwd_hi[...], maps) + dot(fwd_lo[...], maps)
        passing[s] = jnp.exp(-paths[:LINES])
        mu = paths[LINES:]
        mu_hi, mu_lo = split(mu)
        before = dot(mu_hi, tri[...]) + dot(mu_lo, tri[...])
        total = jnp.sum(mu, axis=1, keepdims=True)
        beams[s, 0] = jnp.exp(-scale * before)
        beams[s, 1] = jnp.exp(-scale * (total - before - mu))

        def put(rows, values, sums):
            merged = jnp.zeros((rows.stop - rows.start, 128), f32)
            for odd_side in range(2):
                for back in range(2):
                    k = 2 * back + odd_side
                    flux = jnp.sum(values[odd_side][back], axis=1, keepdims=True)
                    merged = jnp.where(lane == k, flux, merged)
                    merged = jnp.where(lane == views + k, sums[odd_side], merged)
            column[s, rows, :] = merged

        for e in range(E):
            amount = own[s, e].astype(f32)
            values = []
            for odd_side in range(2):
                lit = amount * passing[s, odd_side * SIDE + e * R:odd_side * SIDE + (e + 1) * R]
                values.append([lit * beams[s, back, :R] for back in range(2)])
            put(slice(e * R, (e + 1) * R), values, (total[:R], total[:R]))
        for i in range(E // 2):
            values = []
            both = []
            for odd_side, ref in ((0, low), (1, high)):
                start = odd_side * SIDE + OWN + i * 2 * H
                lit = ref[s, i].astype(f32) * passing[s, start:start + 2 * H]
                rows = slice(R + odd_side * H, R + (odd_side + 1) * H)
                values.append([lit * jnp.concatenate([beams[s, back, rows]] * 2, axis=0) for back in range(2)])
                both.append(jnp.concatenate([total[rows]] * 2, axis=0))
            put(slice(OWN + i * 2 * H, OWN + (i + 1) * 2 * H), values, both)

        part[s, 0] = jnp.transpose(column[s])[:2 * views]
        for k in range(1, views):
            part_copy(s, k).start()

    for k in range(1, views):
        tab_copy(k).wait()
    view_row = iota((views, 1), 0)
    ahead_rows = view_row < 2
    owner = [lax.rem(block + views - k, views) for k in range(views)]
    for s in range(S):
        sums = jnp.zeros((views, 2 * OWN), f32)
        counts = jnp.zeros((views, 2 * OWN), f32)
        for k in range(views):
            here = view_row == owner[k]
            sums = jnp.where(here, tab[k, s:s + 1, :], sums)
            counts = jnp.where(here, tab[k, S + s:S + s + 1, :], counts)
        for k in range(1, views):
            part_copy(s, k).wait()
        blocks, scales = [], []
        for k in range(views):
            offset = jnp.zeros((views, 2 * OWN), f32)
            for j in range(views):
                if j != k:
                    counted = (ahead_rows & (owner[j] < owner[k])) | (~ahead_rows & (owner[j] > owner[k]))
                    offset = offset + jnp.where(counted, part[s, j, views:2 * views, :], 0.0)
            factor = jnp.exp(-scale * offset)
            scales.append(factor)
            blocks.append(part[s, k, 0:views, :] * factor)
        fluor = (blocks[0] + blocks[1] + blocks[2] + blocks[3]) * scale
        fluor_hi, fluor_lo = split(fluor)
        mixed = dot(fluor_hi, gram_hi[...]) + dot(fluor_lo, gram_hi[...]) + dot(fluor_hi, gram_lo[...])
        pulled = counts * mixed - sums
        later = jnp.zeros((views, 2 * OWN), f32)
        for k in range(views):
            counted = (ahead_rows & (owner[k] >= block)) | (~ahead_rows & (owner[k] < block))
            later = later + jnp.where(counted, blocks[k], 0.0)
        stack[0:views, :] = pulled * scales[0]
        stack[views:2 * views, :] = -pulled * later
        pad = jnp.zeros((128 - 2 * views, 2 * OWN), f32)
        column[s] = jnp.transpose(jnp.concatenate([stack[...], pad], axis=0))

        carry = column[s, 0:R, :]
        for e in range(1, E):
            carry = carry + column[s, e * R:(e + 1) * R, :]

        beam = [beams[s, 0, :R], beams[s, 1, :R]]
        seen = [jnp.zeros((R, width), f32), jnp.zeros((R, width), f32)]
        for e in range(E):
            amount = own[s, e].astype(f32)
            cols = column[s, e * R:(e + 1) * R, :]
            direct = None
            for odd_side in range(2):
                start = odd_side * SIDE + e * R
                through = passing[s, start:start + R]
                ahead_pull = cols[:, odd_side:odd_side + 1]
                back_pull = cols[:, 2 + odd_side:2 + odd_side + 1]
                term = through * (ahead_pull * beam[0] + back_pull * beam[1])
                lit = amount * through
                seen[0] = seen[0] + lit * ahead_pull
                seen[1] = seen[1] + lit * back_pull
                weights[0, start:start + R], weights[1, start:start + R] = split(amount * term)
                direct = term if direct is None else direct + term
            result[s, e] = direct
        for i in range(E // 2):
            cols = column[s, OWN + i * 2 * H:OWN + (i + 1) * 2 * H, :]
            for odd_side, ref in ((0, low), (1, high)):
                start = odd_side * SIDE + OWN + i * 2 * H
                rows = slice(R + odd_side * H, R + (odd_side + 1) * H)
                beam_h = [jnp.concatenate([beams[s, back, rows]] * 2, axis=0) for back in range(2)]
                ahead_pull = cols[:, odd_side:odd_side + 1]
                back_pull = cols[:, 2 + odd_side:2 + odd_side + 1]
                term = passing[s, start:start + 2 * H] * (ahead_pull * beam_h[0] + back_pull * beam_h[1])
                weights[0, start:start + 2 * H], weights[1, start:start + 2 * H] = split(ref[s, i].astype(f32) * term)
        lines = dot(back_hi[...], weights[0]) + dot(back_lo[...], weights[0]) + dot(back_hi[...], weights[1])
        ahead_sum = beam[0] * seen[0]
        back_sum = beam[1] * seen[1]
        diff_hi, diff_lo = split(ahead_sum - back_sum)
        chosen = (lane >= views) & (lane < 2 * views)
        extra = jnp.sum(jnp.where(chosen, carry, 0.0), axis=1, keepdims=True)
        back_beam = scale * (dot(diff_hi, tri[...]) + dot(diff_lo, tri[...]) + ahead_sum + extra)
        for e in range(E):
            result[s, e] = result[s, e] + beam_ref[e] * back_beam - lines[e * R:(e + 1) * R]
        pltpu.make_async_copy(result.at[s], out_ref.at[:, s], out_sem.at[s]).start()

    for s in range(S):
        pltpu.make_async_copy(result.at[s], out_ref.at[:, s], out_sem.at[s]).wait()

        @pl.when(me < slabs - 1)
        def _():
            halo(s, True).wait_send()

        @pl.when(me > 0)
        def _():
            halo(s, False).wait_send()


def local(slabs, views, conc, spectra, path_slab, line_offset, profile, beam_absorb, line_absorb):
    cells = conc.shape[-1]
    width = cells // views
    inputs = (conc, spectra, path_slab.reshape(1, -1), line_offset, profile, beam_absorb, line_absorb)
    dma = pltpu.SemaphoreType.DMA
    return pl.pallas_call(
        functools.partial(kernel, slabs, views, cells),
        out_shape=jax.ShapeDtypeStruct((E, S, R, width), f32),
        in_specs=[pl.BlockSpec(memory_space=pltpu.HBM)] * len(inputs),
        out_specs=pl.BlockSpec(memory_space=pltpu.HBM),
        scratch_shapes=[
            pltpu.SMEM(x.shape, x.dtype) if x is beam_absorb else pltpu.VMEM(x.shape, x.dtype) for x in inputs[1:]
        ] + [
            pltpu.VMEM((S, E, R, width), bf16),
            pltpu.VMEM((S, E // 2, 2 * H, width), bf16),
            pltpu.VMEM((S, E // 2, 2 * H, width), bf16),
            pltpu.VMEM((S, E // 2, 2 * H, width), bf16),
            pltpu.VMEM((S, E // 2, 2 * H, width), bf16),
            pltpu.VMEM((LINES + 2 * R, 2 * OWN), bf16),
            pltpu.VMEM((LINES + 2 * R, 2 * OWN), bf16),
            pltpu.VMEM((OWN, LINES), bf16),
            pltpu.VMEM((OWN, LINES), bf16),
            pltpu.VMEM((width, width), bf16),
            pltpu.VMEM((2 * OWN, 2 * OWN), bf16),
            pltpu.VMEM((2 * OWN, 2 * OWN), bf16),
            pltpu.VMEM((S, LINES, width), f32),
            pltpu.VMEM((S, 2, 2 * R, width), f32),
            pltpu.VMEM((2, LINES, width), bf16),
            pltpu.VMEM((slabs, 8, 2 * OWN), f32),
            pltpu.VMEM((slabs, 8, 2 * OWN), f32),
            pltpu.VMEM((views, 8, 2 * OWN), f32),
            pltpu.VMEM((S, views, 2 * views, 2 * OWN), f32),
            pltpu.VMEM((S, 2 * OWN, 128), f32),
            pltpu.VMEM((2 * views, 2 * OWN), f32),
            pltpu.VMEM((S, E, R, width), f32),
            dma((S,)),
            dma((len(inputs) - 1,)),
            dma((S,)),
            dma((2, S)),
            dma((2, S)),
            dma((slabs,)),
            dma((slabs,)),
            dma((views,)),
            dma((views,)),
            dma((S, views)),
            dma((S, views)),
        ],
        compiler_params=pltpu.CompilerParams(
            collective_id=0, has_side_effects=True, vmem_limit_bytes=63 * 1024 * 1024),
    )(*inputs)


def solution(mesh):
    slabs, views = mesh.shape["slab"], mesh.shape["ang"]
    in_specs = (
        P(None, None, "slab", None),
        P("ang", "slab", None),
        P("ang", "slab", None),
        P("ang", "slab"),
        P(),
        P(),
        P(),
    )
    out_specs = P(None, None, "slab", "ang")
    return jax.shard_map(functools.partial(local, slabs, views), mesh=mesh, in_specs=in_specs, out_specs=out_specs,
                         check_vma=False)
```

```python
import functools

import jax
import jax.numpy as jnp
from jax import lax
from jax.experimental import pallas as pl
from jax.experimental.pallas import tpu as pltpu
from jax.sharding import PartitionSpec as P

f32, bf16, i32 = jnp.float32, jnp.bfloat16, jnp.int32
highest = lax.Precision.HIGHEST
MESH = pl.DeviceIdType.MESH

E, S, R, H = 8, 2, 16, 8
OWN, HALO = E * R, E * H
SIDE = OWN + HALO
LINES = 2 * SIDE


def iota(shape, dim):
    return lax.broadcasted_iota(i32, shape, dim)


def split(x):
    hi = x.astype(bf16)
    return hi, (x - hi.astype(f32)).astype(bf16)


def dot(a, b, precision=None):
    return jnp.dot(a, b, precision=precision, preferred_element_type=f32)


def side_index(index):
    own = index < OWN
    rest = index - OWN
    high = index >= SIDE
    element = jnp.where(own, index >> 4, (rest & (HALO - 1)) >> 3)
    row = jnp.where(own, index & (R - 1), jnp.where(high, R, -H) + (index & (H - 1)))
    return element, row


def line_index(index):
    odd = index >= SIDE
    local = jnp.where(odd, index - SIDE, index)
    own = local < OWN
    element = jnp.where(own, local >> 4, (local - OWN) >> 3)
    row = jnp.where(own, local & (R - 1), jnp.where(odd, R, -H) + (local & (H - 1)))
    return odd, element, row


def kernel(slabs, views, cells, conc_ref, *refs):
    small_in, out_ref, small_refs, rest = refs[:6], refs[6], refs[7:13], refs[13:]
    spectra_ref, dest_ref, offset_ref, profile_ref, beam_ref, absorb_ref = small_refs
    (own, low, high, low_out, high_out, fwd_hi, fwd_lo, back_hi, back_lo, tri, gram_hi, gram_lo,
     passing, beams, weights, ray_send, ray_recv, tab, part, column, stack, load_sem, small_sem,
     halo_send_sem, halo_recv_sem, ray_send_sem, ray_recv_sem, tab_send_sem, tab_recv_sem,
     part_send_sem, part_recv_sem) = rest
    me, block = lax.axis_index("slab"), lax.axis_index("ang")
    width = cells // views
    scale = 1.0 / cells

    loads = []
    for s in range(S):
        copy = pltpu.make_async_copy(
            conc_ref.at[:, s, :, pl.ds(pl.multiple_of(block * width, 128), width)], own.at[s], load_sem.at[s])
        copy.start()
        loads.append(copy)
    small_loads = []
    for i in range(6):
        copy = pltpu.make_async_copy(small_in[i], small_refs[i], small_sem.at[i])
        copy.start()
        small_loads.append(copy)

    barrier = pltpu.get_barrier_semaphore()

    def greet(k, carry):
        pl.semaphore_signal(barrier, inc=1, device_id={"slab": lax.rem(me + k, slabs), "ang": block}, device_id_type=MESH)
        return carry

    lax.fori_loop(1, slabs, greet, 0)
    for k in range(1, views):
        pl.semaphore_signal(barrier, inc=1, device_id={"slab": me, "ang": lax.rem(block + k, views)}, device_id_type=MESH)

    @pl.when(me == 0)
    def _():
        low[...] = jnp.zeros_like(low)

    @pl.when(me == slabs - 1)
    def _():
        high[...] = jnp.zeros_like(high)

    def halo(s, upward):
        if upward:
            src, dst, target = high_out, low, me + 1
        else:
            src, dst, target = low_out, high, me - 1
        return pltpu.make_async_remote_copy(
            src_ref=src.at[s], dst_ref=dst.at[s],
            send_sem=halo_send_sem.at[int(upward), s], recv_sem=halo_recv_sem.at[int(upward), s],
            device_id={"slab": target, "ang": block}, device_id_type=MESH)

    for s in range(S):
        loads[s].wait()
        for i in range(E // 2):
            first = own[s, 2 * i].astype(f32)
            second = own[s, 2 * i + 1].astype(f32)
            low_out[s, i] = jnp.concatenate([first[:H], second[:H]], axis=0).astype(bf16)
            high_out[s, i] = jnp.concatenate([first[H:], second[H:]], axis=0).astype(bf16)
        if s == 0:
            pl.semaphore_wait(barrier, slabs - 1 + views - 1)

        @pl.when(me < slabs - 1)
        def _():
            halo(s, True).start()

        @pl.when(me > 0)
        def _():
            halo(s, False).start()

    for copy in small_loads:
        copy.wait()
    lanes = iota((1, 2 * OWN), 1)
    lane_element, _ = side_index(lanes)
    spread = (iota((E, 2 * OWN), 0) == lane_element).astype(f32)
    profile = profile_ref[...]
    flat = (((1,), (1,)), ((), ()))
    lines_of = sum(lax.dot_general(spectra_ref[0], piece, flat, preferred_element_type=f32) for piece in split(profile))
    rays = lines_of.shape[0]
    expanded = [dot(piece, spread.astype(bf16)) for piece in split(lines_of)]
    offsets = offset_ref[...]
    diagonal = iota((rays, rays), 0) == iota((rays, rays), 1)
    ray_row = (dest_ref[...] << 4) + (offsets & (R - 1))
    ray_row = jnp.sum(jnp.where(diagonal, ray_row, 0).astype(f32), axis=1, keepdims=True).astype(i32)
    odd_view = block % 2
    halo_row = jnp.where(odd_view == 1, R, -H) + (lanes & (H - 1))
    lane_row = jnp.where(lanes < OWN, lanes & (R - 1), jnp.where(lanes < SIDE, halo_row, -(1 << 24)))
    ray_gap = ray_row - lane_row
    row8 = iota((8, rays), 0)
    ray_slice = offsets >> 4
    pick_sum = jnp.where(ray_slice == row8, 1.0, 0.0)
    pick_count = jnp.where(ray_slice == row8 - S, 1.0, 0.0)
    pick = jnp.concatenate([pick_sum, pick_sum, pick_count, jnp.zeros_like(pick_sum)], axis=1).astype(bf16)

    def message(target):
        hit = ray_gap == target * R
        picked = [jnp.where(hit, x, 0.0) for x in (*expanded, 1.0)]
        return dot(pick, jnp.concatenate(picked + [jnp.zeros_like(picked[0])], axis=0).astype(bf16))

    def ray_copy(k):
        return pltpu.make_async_remote_copy(
            src_ref=ray_send.at[k], dst_ref=ray_recv.at[k], send_sem=ray_send_sem.at[k], recv_sem=ray_recv_sem.at[k],
            device_id={"slab": lax.rem(me + k, slabs), "ang": block}, device_id_type=MESH)

    def send_rays(k, carry):
        ray_send[k] = message(lax.rem(me + k, slabs))
        ray_copy(k).start()
        return carry

    lax.fori_loop(1, slabs, send_rays, 0)
    mine = message(me)

    m_index = iota((LINES, 1), 0)
    odd, m_element, m_row = line_index(m_index)
    k_index = iota((1, 2 * OWN), 1)
    k_element, k_row = side_index(k_index)
    ahead = jnp.where(odd, m_row - k_row, k_row - m_row)
    band = (ahead >= 1) & (ahead <= H)
    rows_hot = (m_element == iota((LINES, E), 1)).astype(bf16)
    cols_hot = spread.astype(bf16)
    absorb = absorb_ref[...]
    for piece, ref in zip(split(absorb), (fwd_hi, fwd_lo)):
        mixed = dot(dot(rows_hot, piece).astype(bf16), cols_hot)
        ref[:LINES] = jnp.where(band, mixed, 0.0).astype(bf16)
    b_row = jnp.zeros((1, 2 * OWN), f32)
    for e in range(E):
        b_row = jnp.where(k_element == e, beam_ref[e], b_row)
    beam_rows = iota((2 * R, 1), 0)
    beam_row = jnp.where(beam_rows < R, beam_rows, jnp.where(beam_rows < R + H, beam_rows - R - H, beam_rows - H))
    beam_mat = jnp.where(beam_row == k_row, b_row, 0.0)
    fwd_hi[LINES:], fwd_lo[LINES:] = split(beam_mat)

    n_index = iota((1, LINES), 1)
    n_odd, n_element, n_row = line_index(n_index)
    o_index = iota((OWN, 1), 0)
    o_element, o_row = o_index >> 4, o_index & (R - 1)
    ahead = jnp.where(n_odd, n_row - o_row, o_row - n_row)
    band = (ahead >= 1) & (ahead <= H)
    rows_hot = (o_element == iota((OWN, E), 1)).astype(bf16)
    cols_hot = (iota((E, LINES), 0) == n_element).astype(bf16)
    for piece, ref in zip(split(absorb), (back_hi, back_lo)):
        left = lax.dot_general(rows_hot, piece, (((1,), (1,)), ((), ())), preferred_element_type=f32)
        ref[...] = jnp.where(band, dot(left.astype(bf16), cols_hot), 0.0).astype(bf16)

    tri[...] = jnp.where(iota((width, width), 0) < iota((width, width), 1), 1.0, 0.0).astype(bf16)

    small = lax.dot_general(profile, profile, flat, precision=highest, preferred_element_type=f32)
    g_rows = iota((2 * OWN, 1), 0)
    g_element, g_row = side_index(g_rows)
    g_hot = (g_element == iota((2 * OWN, E), 1)).astype(bf16)
    for piece, ref in zip(split(small), (gram_hi, gram_lo)):
        wide = dot(dot(g_hot, piece).astype(bf16), spread.astype(bf16))
        ref[...] = jnp.where(g_row == k_row, wide, 0.0).astype(bf16)

    def gather_rays(k, total):
        ray_copy(k).wait()
        return total + ray_recv[k]

    def to_view(src, dst, k, send, recv):
        return pltpu.make_async_remote_copy(
            src_ref=src, dst_ref=dst, send_sem=send, recv_sem=recv,
            device_id={"slab": me, "ang": lax.rem(block + k, views)}, device_id_type=MESH)

    def tab_copy(k):
        return to_view(tab.at[0], tab.at[k], k, tab_send_sem.at[k], tab_recv_sem.at[k])

    def part_copy(s, k):
        return to_view(part.at[s, 0], part.at[s, k], k, part_send_sem.at[s, k], part_recv_sem.at[s, k])

    lane = iota((1, 128), 1)
    column[:, SIDE:, :] = jnp.zeros((S, 2 * OWN - SIDE, 128), f32)
    for s in range(S):
        @pl.when(me > 0)
        def _():
            halo(s, True).wait_recv()

        @pl.when(me < slabs - 1)
        def _():
            halo(s, False).wait_recv()

        if s == S - 1:
            tab[0] = lax.fori_loop(1, slabs, gather_rays, mine)
            for k in range(1, views):
                tab_copy(k).start()

        maps = jnp.concatenate([own[s], low[s], high[s]], axis=0).reshape(2 * OWN, width)
        paths = dot(fwd_hi[...], maps) + dot(fwd_lo[...], maps)
        passing[s] = jnp.exp(-paths[:LINES])
        mu = paths[LINES:]
        mu_hi, mu_lo = split(mu)
        before = dot(mu_hi, tri[...]) + dot(mu_lo, tri[...])
        total = jnp.sum(mu, axis=1, keepdims=True)
        beams[s, 0] = jnp.exp(-scale * before)
        beams[s, 1] = jnp.exp(-scale * (total - before - mu))

        def put(rows, values, sums):
            merged = jnp.zeros((rows.stop - rows.start, 128), f32)
            for odd_side in range(2):
                for back in range(2):
                    k = 2 * back + odd_side
                    flux = jnp.sum(values[odd_side][back], axis=1, keepdims=True)
                    merged = jnp.where(lane == k, flux, merged)
                    merged = jnp.where(lane == views + k, sums[odd_side], merged)
            column[s, rows, :] = merged

        for e in range(E):
            amount = own[s, e].astype(f32)
            values = []
            for odd_side in range(2):
                lit = amount * passing[s, odd_side * SIDE + e * R:odd_side * SIDE + (e + 1) * R]
                values.append([lit * beams[s, back, :R] for back in range(2)])
            put(slice(e * R, (e + 1) * R), values, (total[:R], total[:R]))
        for i in range(E // 2):
            values = []
            both = []
            for odd_side, ref in ((0, low), (1, high)):
                start = odd_side * SIDE + OWN + i * 2 * H
                lit = ref[s, i].astype(f32) * passing[s, start:start + 2 * H]
                rows = slice(R + odd_side * H, R + (odd_side + 1) * H)
                values.append([lit * jnp.concatenate([beams[s, back, rows]] * 2, axis=0) for back in range(2)])
                both.append(jnp.concatenate([total[rows]] * 2, axis=0))
            put(slice(OWN + i * 2 * H, OWN + (i + 1) * 2 * H), values, both)

        part[s, 0] = jnp.transpose(column[s])[:2 * views]
        for k in range(1, views):
            part_copy(s, k).start()

    for k in range(1, views):
        tab_copy(k).wait()
    view_row = iota((views, 1), 0)
    ahead_rows = view_row < 2
    owner = [lax.rem(block + views - k, views) for k in range(views)]
    for s in range(S):
        sums = jnp.zeros((views, 2 * OWN), f32)
        counts = jnp.zeros((views, 2 * OWN), f32)
        for k in range(views):
            here = view_row == owner[k]
            sums = jnp.where(here, tab[k, s:s + 1, :], sums)
            counts = jnp.where(here, tab[k, S + s:S + s + 1, :], counts)
        for k in range(1, views):
            part_copy(s, k).wait()
        blocks, scales = [], []
        for k in range(views):
            offset = jnp.zeros((views, 2 * OWN), f32)
            for j in range(views):
                if j != k:
                    counted = (ahead_rows & (owner[j] < owner[k])) | (~ahead_rows & (owner[j] > owner[k]))
                    offset = offset + jnp.where(counted, part[s, j, views:2 * views, :], 0.0)
            factor = jnp.exp(-scale * offset)
            scales.append(factor)
            blocks.append(part[s, k, 0:views, :] * factor)
        fluor = (blocks[0] + blocks[1] + blocks[2] + blocks[3]) * scale
        fluor_hi, fluor_lo = split(fluor)
        mixed = dot(fluor_hi, gram_hi[...]) + dot(fluor_lo, gram_hi[...]) + dot(fluor_hi, gram_lo[...])
        pulled = counts * mixed - sums
        later = jnp.zeros((views, 2 * OWN), f32)
        for k in range(views):
            counted = (ahead_rows & (owner[k] >= block)) | (~ahead_rows & (owner[k] < block))
            later = later + jnp.where(counted, blocks[k], 0.0)
        stack[0:views, :] = pulled * scales[0]
        stack[views:2 * views, :] = -pulled * later
        pad = jnp.zeros((128 - 2 * views, 2 * OWN), f32)
        column[s] = jnp.transpose(jnp.concatenate([stack[...], pad], axis=0))

        carry = column[s, 0:R, :]
        for e in range(1, E):
            carry = carry + column[s, e * R:(e + 1) * R, :]

        beam = [beams[s, 0, :R], beams[s, 1, :R]]
        seen = [jnp.zeros((R, width), f32), jnp.zeros((R, width), f32)]
        for e in range(E):
            amount = own[s, e].astype(f32)
            cols = column[s, e * R:(e + 1) * R, :]
            direct = None
            for odd_side in range(2):
                start = odd_side * SIDE + e * R
                through = passing[s, start:start + R]
                ahead_pull = cols[:, odd_side:odd_side + 1]
                back_pull = cols[:, 2 + odd_side:2 + odd_side + 1]
                term = through * (ahead_pull * beam[0] + back_pull * beam[1])
                lit = amount * through
                seen[0] = seen[0] + lit * ahead_pull
                seen[1] = seen[1] + lit * back_pull
                weights[0, start:start + R], weights[1, start:start + R] = split(amount * term)
                direct = term if direct is None else direct + term
            out_ref[e, s] = direct
        for i in range(E // 2):
            cols = column[s, OWN + i * 2 * H:OWN + (i + 1) * 2 * H, :]
            for odd_side, ref in ((0, low), (1, high)):
                start = odd_side * SIDE + OWN + i * 2 * H
                rows = slice(R + odd_side * H, R + (odd_side + 1) * H)
                beam_h = [jnp.concatenate([beams[s, back, rows]] * 2, axis=0) for back in range(2)]
                ahead_pull = cols[:, odd_side:odd_side + 1]
                back_pull = cols[:, 2 + odd_side:2 + odd_side + 1]
                term = passing[s, start:start + 2 * H] * (ahead_pull * beam_h[0] + back_pull * beam_h[1])
                weights[0, start:start + 2 * H], weights[1, start:start + 2 * H] = split(ref[s, i].astype(f32) * term)
        lines = dot(back_hi[...], weights[0]) + dot(back_lo[...], weights[0]) + dot(back_hi[...], weights[1])
        ahead_sum = beam[0] * seen[0]
        back_sum = beam[1] * seen[1]
        diff_hi, diff_lo = split(ahead_sum - back_sum)
        chosen = (lane >= views) & (lane < 2 * views)
        extra = jnp.sum(jnp.where(chosen, carry, 0.0), axis=1, keepdims=True)
        back_beam = scale * (dot(diff_hi, tri[...]) + dot(diff_lo, tri[...]) + ahead_sum + extra)
        for e in range(E):
            out_ref[e, s] = out_ref[e, s] + beam_ref[e] * back_beam - lines[e * R:(e + 1) * R]

        @pl.when(me < slabs - 1)
        def _():
            halo(s, True).wait_send()

        @pl.when(me > 0)
        def _():
            halo(s, False).wait_send()


def local(slabs, views, conc, spectra, path_slab, line_offset, profile, beam_absorb, line_absorb):
    cells = conc.shape[-1]
    width = cells // views
    inputs = (conc, spectra, path_slab.reshape(1, -1), line_offset, profile, beam_absorb, line_absorb)
    dma = pltpu.SemaphoreType.DMA
    return pl.pallas_call(
        functools.partial(kernel, slabs, views, cells),
        out_shape=jax.ShapeDtypeStruct((E, S, R, width), f32),
        in_specs=[pl.BlockSpec(memory_space=pltpu.HBM)] * len(inputs),
        out_specs=pl.BlockSpec(memory_space=pltpu.VMEM),
        scratch_shapes=[
            pltpu.SMEM(x.shape, x.dtype) if x is beam_absorb else pltpu.VMEM(x.shape, x.dtype) for x in inputs[1:]
        ] + [
            pltpu.VMEM((S, E, R, width), bf16),
            pltpu.VMEM((S, E // 2, 2 * H, width), bf16),
            pltpu.VMEM((S, E // 2, 2 * H, width), bf16),
            pltpu.VMEM((S, E // 2, 2 * H, width), bf16),
            pltpu.VMEM((S, E // 2, 2 * H, width), bf16),
            pltpu.VMEM((LINES + 2 * R, 2 * OWN), bf16),
            pltpu.VMEM((LINES + 2 * R, 2 * OWN), bf16),
            pltpu.VMEM((OWN, LINES), bf16),
            pltpu.VMEM((OWN, LINES), bf16),
            pltpu.VMEM((width, width), bf16),
            pltpu.VMEM((2 * OWN, 2 * OWN), bf16),
            pltpu.VMEM((2 * OWN, 2 * OWN), bf16),
            pltpu.VMEM((S, LINES, width), f32),
            pltpu.VMEM((S, 2, 2 * R, width), f32),
            pltpu.VMEM((2, LINES, width), bf16),
            pltpu.VMEM((slabs, 8, 2 * OWN), f32),
            pltpu.VMEM((slabs, 8, 2 * OWN), f32),
            pltpu.VMEM((views, 8, 2 * OWN), f32),
            pltpu.VMEM((S, views, 2 * views, 2 * OWN), f32),
            pltpu.VMEM((S, 2 * OWN, 128), f32),
            pltpu.VMEM((2 * views, 2 * OWN), f32),
            dma((S,)),
            dma((len(inputs) - 1,)),
            dma((2, S)),
            dma((2, S)),
            dma((slabs,)),
            dma((slabs,)),
            dma((views,)),
            dma((views,)),
            dma((S, views)),
            dma((S, views)),
        ],
        compiler_params=pltpu.CompilerParams(
            collective_id=0, has_side_effects=True, vmem_limit_bytes=40 * 1024 * 1024),
    )(*[pltpu.with_memory_space_constraint(x, pltpu.HBM) for x in inputs])


def solution(mesh):
    slabs, views = mesh.shape["slab"], mesh.shape["ang"]
    in_specs = (
        P(None, None, "slab", None),
        P("ang", "slab", None),
        P("ang", "slab", None),
        P("ang", "slab"),
        P(),
        P(),
        P(),
    )
    out_specs = P(None, None, "slab", "ang")
    return jax.shard_map(functools.partial(local, slabs, views), mesh=mesh, in_specs=in_specs, out_specs=out_specs,
                         check_vma=False)
```

```python
import functools

import jax
import jax.numpy as jnp
from jax import lax
from jax.experimental import pallas as pl
from jax.experimental.pallas import tpu as pltpu
from jax.sharding import PartitionSpec as P

f32, bf16, i32 = jnp.float32, jnp.bfloat16, jnp.int32
highest = lax.Precision.HIGHEST
MESH = pl.DeviceIdType.MESH

E, S, R, H = 8, 2, 16, 8
OWN, HALO = E * R, E * H
SIDE = OWN + HALO
LINES = 2 * SIDE


def iota(shape, dim):
    return lax.broadcasted_iota(i32, shape, dim)


def split(x):
    hi = x.astype(bf16)
    return hi, (x - hi.astype(f32)).astype(bf16)


def dot(a, b, precision=None):
    return jnp.dot(a, b, precision=precision, preferred_element_type=f32)


def side_index(index):
    own = index < OWN
    rest = index - OWN
    high = index >= SIDE
    element = jnp.where(own, index >> 4, (rest & (HALO - 1)) >> 3)
    row = jnp.where(own, index & (R - 1), jnp.where(high, R, -H) + (index & (H - 1)))
    return element, row


def line_index(index):
    odd = index >= SIDE
    local = jnp.where(odd, index - SIDE, index)
    own = local < OWN
    element = jnp.where(own, local >> 4, (local - OWN) >> 3)
    row = jnp.where(own, local & (R - 1), jnp.where(odd, R, -H) + (local & (H - 1)))
    return odd, element, row


def kernel(slabs, views, cells, conc_ref, *refs):
    small_in, out_ref, small_refs, rest = refs[:6], refs[6], refs[7:13], refs[13:]
    spectra_ref, dest_ref, offset_ref, profile_ref, beam_ref, absorb_ref = small_refs
    (own, low, high, low_out, high_out, fwd_hi, fwd_lo, back_hi, back_lo, tri, gram_hi, gram_lo,
     passing, beams, weights, ray_send, ray_recv, tab, part, column, stack, load_sem, small_sem,
     halo_send_sem, halo_recv_sem, ray_send_sem, ray_recv_sem, tab_send_sem, tab_recv_sem,
     part_send_sem, part_recv_sem) = rest
    me, block = lax.axis_index("slab"), lax.axis_index("ang")
    width = cells // views
    scale = 1.0 / cells

    loads = []
    for s in range(S):
        copy = pltpu.make_async_copy(
            conc_ref.at[:, s, :, pl.ds(pl.multiple_of(block * width, 128), width)], own.at[s], load_sem.at[s])
        copy.start()
        loads.append(copy)
    barrier = pltpu.get_barrier_semaphore()

    def greet(k, carry):
        pl.semaphore_signal(barrier, inc=1, device_id={"slab": lax.rem(me + k, slabs), "ang": block}, device_id_type=MESH)
        return carry

    lax.fori_loop(1, slabs, greet, 0)
    for k in range(1, views):
        pl.semaphore_signal(barrier, inc=1, device_id={"slab": me, "ang": lax.rem(block + k, views)}, device_id_type=MESH)

    small_loads = []
    for i in range(6):
        copy = pltpu.make_async_copy(small_in[i], small_refs[i], small_sem.at[i])
        copy.start()
        small_loads.append(copy)

    @pl.when(me == 0)
    def _():
        low[...] = jnp.zeros_like(low)

    @pl.when(me == slabs - 1)
    def _():
        high[...] = jnp.zeros_like(high)

    def halo(s, upward):
        if upward:
            src, dst, target = high_out, low, me + 1
        else:
            src, dst, target = low_out, high, me - 1
        return pltpu.make_async_remote_copy(
            src_ref=src.at[s], dst_ref=dst.at[s],
            send_sem=halo_send_sem.at[int(upward), s], recv_sem=halo_recv_sem.at[int(upward), s],
            device_id={"slab": target, "ang": block}, device_id_type=MESH)

    for s in range(S):
        loads[s].wait()
        for i in range(E // 2):
            first = own[s, 2 * i].astype(f32)
            second = own[s, 2 * i + 1].astype(f32)
            low_out[s, i] = jnp.concatenate([first[:H], second[:H]], axis=0).astype(bf16)
            high_out[s, i] = jnp.concatenate([first[H:], second[H:]], axis=0).astype(bf16)
        if s == 0:
            pl.semaphore_wait(barrier, slabs - 1 + views - 1)

        @pl.when(me < slabs - 1)
        def _():
            halo(s, True).start()

        @pl.when(me > 0)
        def _():
            halo(s, False).start()

    for copy in small_loads:
        copy.wait()
    lanes = iota((1, 2 * OWN), 1)
    lane_element, _ = side_index(lanes)
    spread = (iota((E, 2 * OWN), 0) == lane_element).astype(f32)
    profile = profile_ref[...]
    flat = (((1,), (1,)), ((), ()))
    lines_of = sum(lax.dot_general(spectra_ref[0], piece, flat, preferred_element_type=f32) for piece in split(profile))
    rays = lines_of.shape[0]
    expanded = [dot(piece, spread.astype(bf16)) for piece in split(lines_of)]
    offsets = offset_ref[...]
    diagonal = iota((rays, rays), 0) == iota((rays, rays), 1)
    ray_row = (dest_ref[...] << 4) + (offsets & (R - 1))
    ray_row = jnp.sum(jnp.where(diagonal, ray_row, 0).astype(f32), axis=1, keepdims=True).astype(i32)
    odd_view = block % 2
    halo_row = jnp.where(odd_view == 1, R, -H) + (lanes & (H - 1))
    lane_row = jnp.where(lanes < OWN, lanes & (R - 1), jnp.where(lanes < SIDE, halo_row, -(1 << 24)))
    ray_gap = ray_row - lane_row
    row8 = iota((8, rays), 0)
    ray_slice = offsets >> 4
    pick_sum = jnp.where(ray_slice == row8, 1.0, 0.0)
    pick_count = jnp.where(ray_slice == row8 - S, 1.0, 0.0)
    pick = jnp.concatenate([pick_sum, pick_sum, pick_count, jnp.zeros_like(pick_sum)], axis=1).astype(bf16)

    def message(target):
        hit = ray_gap == target * R
        picked = [jnp.where(hit, x, 0.0) for x in (*expanded, 1.0)]
        return dot(pick, jnp.concatenate(picked + [jnp.zeros_like(picked[0])], axis=0).astype(bf16))

    def ray_copy(k):
        return pltpu.make_async_remote_copy(
            src_ref=ray_send.at[k], dst_ref=ray_recv.at[k], send_sem=ray_send_sem.at[k], recv_sem=ray_recv_sem.at[k],
            device_id={"slab": lax.rem(me + k, slabs), "ang": block}, device_id_type=MESH)

    def send_rays(k, carry):
        ray_send[k] = message(lax.rem(me + k, slabs))
        ray_copy(k).start()
        return carry

    lax.fori_loop(1, slabs, send_rays, 0)
    mine = message(me)

    m_index = iota((LINES, 1), 0)
    odd, m_element, m_row = line_index(m_index)
    k_index = iota((1, 2 * OWN), 1)
    k_element, k_row = side_index(k_index)
    ahead = jnp.where(odd, m_row - k_row, k_row - m_row)
    band = (ahead >= 1) & (ahead <= H)
    rows_hot = (m_element == iota((LINES, E), 1)).astype(bf16)
    cols_hot = spread.astype(bf16)
    absorb = absorb_ref[...]
    for piece, ref in zip(split(absorb), (fwd_hi, fwd_lo)):
        mixed = dot(dot(rows_hot, piece).astype(bf16), cols_hot)
        ref[:LINES] = jnp.where(band, mixed, 0.0).astype(bf16)
    b_row = jnp.zeros((1, 2 * OWN), f32)
    for e in range(E):
        b_row = jnp.where(k_element == e, beam_ref[e], b_row)
    beam_rows = iota((2 * R, 1), 0)
    beam_row = jnp.where(beam_rows < R, beam_rows, jnp.where(beam_rows < R + H, beam_rows - R - H, beam_rows - H))
    beam_mat = jnp.where(beam_row == k_row, b_row, 0.0)
    fwd_hi[LINES:], fwd_lo[LINES:] = split(beam_mat)

    n_index = iota((1, LINES), 1)
    n_odd, n_element, n_row = line_index(n_index)
    o_index = iota((OWN, 1), 0)
    o_element, o_row = o_index >> 4, o_index & (R - 1)
    ahead = jnp.where(n_odd, n_row - o_row, o_row - n_row)
    band = (ahead >= 1) & (ahead <= H)
    rows_hot = (o_element == iota((OWN, E), 1)).astype(bf16)
    cols_hot = (iota((E, LINES), 0) == n_element).astype(bf16)
    for piece, ref in zip(split(absorb), (back_hi, back_lo)):
        left = lax.dot_general(rows_hot, piece, (((1,), (1,)), ((), ())), preferred_element_type=f32)
        ref[...] = jnp.where(band, dot(left.astype(bf16), cols_hot), 0.0).astype(bf16)

    tri[...] = jnp.where(iota((width, width), 0) < iota((width, width), 1), 1.0, 0.0).astype(bf16)

    small = lax.dot_general(profile, profile, flat, precision=highest, preferred_element_type=f32)
    g_rows = iota((2 * OWN, 1), 0)
    g_element, g_row = side_index(g_rows)
    g_hot = (g_element == iota((2 * OWN, E), 1)).astype(bf16)
    for piece, ref in zip(split(small), (gram_hi, gram_lo)):
        wide = dot(dot(g_hot, piece).astype(bf16), spread.astype(bf16))
        ref[...] = jnp.where(g_row == k_row, wide, 0.0).astype(bf16)

    def gather_rays(k, total):
        ray_copy(k).wait()
        return total + ray_recv[k]

    def to_view(src, dst, k, send, recv):
        return pltpu.make_async_remote_copy(
            src_ref=src, dst_ref=dst, send_sem=send, recv_sem=recv,
            device_id={"slab": me, "ang": lax.rem(block + k, views)}, device_id_type=MESH)

    def tab_copy(k):
        return to_view(tab.at[0], tab.at[k], k, tab_send_sem.at[k], tab_recv_sem.at[k])

    def part_copy(s, k):
        return to_view(part.at[s, 0], part.at[s, k], k, part_send_sem.at[s, k], part_recv_sem.at[s, k])

    lane = iota((1, 128), 1)
    column[:, SIDE:, :] = jnp.zeros((S, 2 * OWN - SIDE, 128), f32)
    for s in range(S):
        @pl.when(me > 0)
        def _():
            halo(s, True).wait_recv()

        @pl.when(me < slabs - 1)
        def _():
            halo(s, False).wait_recv()

        maps = jnp.concatenate([own[s], low[s], high[s]], axis=0).reshape(2 * OWN, width)
        paths = dot(fwd_hi[...], maps) + dot(fwd_lo[...], maps)
        passing[s] = jnp.exp(-paths[:LINES])
        mu = paths[LINES:]
        mu_hi, mu_lo = split(mu)
        before = dot(mu_hi, tri[...]) + dot(mu_lo, tri[...])
        total = jnp.sum(mu, axis=1, keepdims=True)
        beams[s, 0] = jnp.exp(-scale * before)
        beams[s, 1] = jnp.exp(-scale * (total - before - mu))

        if s == S - 1:
            tab[0] = lax.fori_loop(1, slabs, gather_rays, mine)
            for k in range(1, views):
                tab_copy(k).start()

        def put(rows, values, sums):
            merged = jnp.zeros((rows.stop - rows.start, 128), f32)
            for odd_side in range(2):
                for back in range(2):
                    k = 2 * back + odd_side
                    flux = jnp.sum(values[odd_side][back], axis=1, keepdims=True)
                    merged = jnp.where(lane == k, flux, merged)
                    merged = jnp.where(lane == views + k, sums[odd_side], merged)
            column[s, rows, :] = merged

        for e in range(E):
            amount = own[s, e].astype(f32)
            values = []
            for odd_side in range(2):
                lit = amount * passing[s, odd_side * SIDE + e * R:odd_side * SIDE + (e + 1) * R]
                values.append([lit * beams[s, back, :R] for back in range(2)])
            put(slice(e * R, (e + 1) * R), values, (total[:R], total[:R]))
        for i in range(E // 2):
            values = []
            both = []
            for odd_side, ref in ((0, low), (1, high)):
                start = odd_side * SIDE + OWN + i * 2 * H
                lit = ref[s, i].astype(f32) * passing[s, start:start + 2 * H]
                rows = slice(R + odd_side * H, R + (odd_side + 1) * H)
                values.append([lit * jnp.concatenate([beams[s, back, rows]] * 2, axis=0) for back in range(2)])
                both.append(jnp.concatenate([total[rows]] * 2, axis=0))
            put(slice(OWN + i * 2 * H, OWN + (i + 1) * 2 * H), values, both)

        part[s, 0] = jnp.transpose(column[s])[:2 * views]
        for k in range(1, views):
            part_copy(s, k).start()

    for k in range(1, views):
        tab_copy(k).wait()
    view_row = iota((views, 1), 0)
    ahead_rows = view_row < 2
    owner = [lax.rem(block + views - k, views) for k in range(views)]
    for s in range(S):
        sums = jnp.zeros((views, 2 * OWN), f32)
        counts = jnp.zeros((views, 2 * OWN), f32)
        for k in range(views):
            here = view_row == owner[k]
            sums = jnp.where(here, tab[k, s:s + 1, :], sums)
            counts = jnp.where(here, tab[k, S + s:S + s + 1, :], counts)
        for k in range(1, views):
            part_copy(s, k).wait()
        blocks, scales = [], []
        for k in range(views):
            offset = jnp.zeros((views, 2 * OWN), f32)
            for j in range(views):
                if j != k:
                    counted = (ahead_rows & (owner[j] < owner[k])) | (~ahead_rows & (owner[j] > owner[k]))
                    offset = offset + jnp.where(counted, part[s, j, views:2 * views, :], 0.0)
            factor = jnp.exp(-scale * offset)
            scales.append(factor)
            blocks.append(part[s, k, 0:views, :] * factor)
        fluor = (blocks[0] + blocks[1] + blocks[2] + blocks[3]) * scale
        fluor_hi, fluor_lo = split(fluor)
        mixed = dot(fluor_hi, gram_hi[...]) + dot(fluor_lo, gram_hi[...]) + dot(fluor_hi, gram_lo[...])
        pulled = counts * mixed - sums
        later = jnp.zeros((views, 2 * OWN), f32)
        for k in range(views):
            counted = (ahead_rows & (owner[k] >= block)) | (~ahead_rows & (owner[k] < block))
            later = later + jnp.where(counted, blocks[k], 0.0)
        stack[0:views, :] = pulled * scales[0]
        stack[views:2 * views, :] = -pulled * later
        pad = jnp.zeros((128 - 2 * views, 2 * OWN), f32)
        column[s] = jnp.transpose(jnp.concatenate([stack[...], pad], axis=0))

        carry = column[s, 0:R, :]
        for e in range(1, E):
            carry = carry + column[s, e * R:(e + 1) * R, :]

        beam = [beams[s, 0, :R], beams[s, 1, :R]]
        seen = [jnp.zeros((R, width), f32), jnp.zeros((R, width), f32)]
        for e in range(E):
            amount = own[s, e].astype(f32)
            cols = column[s, e * R:(e + 1) * R, :]
            direct = None
            for odd_side in range(2):
                start = odd_side * SIDE + e * R
                through = passing[s, start:start + R]
                ahead_pull = cols[:, odd_side:odd_side + 1]
                back_pull = cols[:, 2 + odd_side:2 + odd_side + 1]
                term = through * (ahead_pull * beam[0] + back_pull * beam[1])
                lit = amount * through
                seen[0] = seen[0] + lit * ahead_pull
                seen[1] = seen[1] + lit * back_pull
                weights[0, start:start + R], weights[1, start:start + R] = split(amount * term)
                direct = term if direct is None else direct + term
            out_ref[e, s] = direct
        for i in range(E // 2):
            cols = column[s, OWN + i * 2 * H:OWN + (i + 1) * 2 * H, :]
            for odd_side, ref in ((0, low), (1, high)):
                start = odd_side * SIDE + OWN + i * 2 * H
                rows = slice(R + odd_side * H, R + (odd_side + 1) * H)
                beam_h = [jnp.concatenate([beams[s, back, rows]] * 2, axis=0) for back in range(2)]
                ahead_pull = cols[:, odd_side:odd_side + 1]
                back_pull = cols[:, 2 + odd_side:2 + odd_side + 1]
                term = passing[s, start:start + 2 * H] * (ahead_pull * beam_h[0] + back_pull * beam_h[1])
                weights[0, start:start + 2 * H], weights[1, start:start + 2 * H] = split(ref[s, i].astype(f32) * term)
        lines = dot(back_hi[...], weights[0]) + dot(back_lo[...], weights[0]) + dot(back_hi[...], weights[1])
        ahead_sum = beam[0] * seen[0]
        back_sum = beam[1] * seen[1]
        diff_hi, diff_lo = split(ahead_sum - back_sum)
        chosen = (lane >= views) & (lane < 2 * views)
        extra = jnp.sum(jnp.where(chosen, carry, 0.0), axis=1, keepdims=True)
        back_beam = scale * (dot(diff_hi, tri[...]) + dot(diff_lo, tri[...]) + ahead_sum + extra)
        for e in range(E):
            out_ref[e, s] = out_ref[e, s] + beam_ref[e] * back_beam - lines[e * R:(e + 1) * R]

        @pl.when(me < slabs - 1)
        def _():
            halo(s, True).wait_send()

        @pl.when(me > 0)
        def _():
            halo(s, False).wait_send()


def local(slabs, views, conc, spectra, path_slab, line_offset, profile, beam_absorb, line_absorb):
    cells = conc.shape[-1]
    width = cells // views
    inputs = (conc, spectra, path_slab.reshape(1, -1), line_offset, profile, beam_absorb, line_absorb)
    dma = pltpu.SemaphoreType.DMA
    return pl.pallas_call(
        functools.partial(kernel, slabs, views, cells),
        out_shape=jax.ShapeDtypeStruct((E, S, R, width), f32),
        in_specs=[pl.BlockSpec(memory_space=pltpu.HBM)] * len(inputs),
        out_specs=pl.BlockSpec(memory_space=pltpu.VMEM),
        scratch_shapes=[
            pltpu.SMEM(x.shape, x.dtype) if x is beam_absorb else pltpu.VMEM(x.shape, x.dtype) for x in inputs[1:]
        ] + [
            pltpu.VMEM((S, E, R, width), bf16),
            pltpu.VMEM((S, E // 2, 2 * H, width), bf16),
            pltpu.VMEM((S, E // 2, 2 * H, width), bf16),
            pltpu.VMEM((S, E // 2, 2 * H, width), bf16),
            pltpu.VMEM((S, E // 2, 2 * H, width), bf16),
            pltpu.VMEM((LINES + 2 * R, 2 * OWN), bf16),
            pltpu.VMEM((LINES + 2 * R, 2 * OWN), bf16),
            pltpu.VMEM((OWN, LINES), bf16),
            pltpu.VMEM((OWN, LINES), bf16),
            pltpu.VMEM((width, width), bf16),
            pltpu.VMEM((2 * OWN, 2 * OWN), bf16),
            pltpu.VMEM((2 * OWN, 2 * OWN), bf16),
            pltpu.VMEM((S, LINES, width), f32),
            pltpu.VMEM((S, 2, 2 * R, width), f32),
            pltpu.VMEM((2, LINES, width), bf16),
            pltpu.VMEM((slabs, 8, 2 * OWN), f32),
            pltpu.VMEM((slabs, 8, 2 * OWN), f32),
            pltpu.VMEM((views, 8, 2 * OWN), f32),
            pltpu.VMEM((S, views, 2 * views, 2 * OWN), f32),
            pltpu.VMEM((S, 2 * OWN, 128), f32),
            pltpu.VMEM((2 * views, 2 * OWN), f32),
            dma((S,)),
            dma((len(inputs) - 1,)),
            dma((2, S)),
            dma((2, S)),
            dma((slabs,)),
            dma((slabs,)),
            dma((views,)),
            dma((views,)),
            dma((S, views)),
            dma((S, views)),
        ],
        compiler_params=pltpu.CompilerParams(
            collective_id=0, has_side_effects=True, vmem_limit_bytes=40 * 1024 * 1024),
    )(*[pltpu.with_memory_space_constraint(x, pltpu.HBM) for x in inputs])


def solution(mesh):
    slabs, views = mesh.shape["slab"], mesh.shape["ang"]
    in_specs = (
        P(None, None, "slab", None),
        P("ang", "slab", None),
        P("ang", "slab", None),
        P("ang", "slab"),
        P(),
        P(),
        P(),
    )
    out_specs = P(None, None, "slab", "ang")
    return jax.shard_map(functools.partial(local, slabs, views), mesh=mesh, in_specs=in_specs, out_specs=out_specs,
                         check_vma=False)
```
